128 devices in a mesh: users: 64 (over z, y, x), mp: 2 (over core).
Axes of the slice: x: 4, y: 4, z: 4, core: 2. Of those that a mesh axis runs over, the one named last changes fastest.
Arguments:
- candidates: bfloat16 [65536, 1024], P('users', 'mp'), may hold values from -6 to 6
- cand_dest: int32 [65536, 1], P('users'), may hold values from 0 to 63; in each aligned block of 1024 rows (0 to 1023, 1024 to 2047, ...) at most 32 rows name the same one
- cand_slot: int32 [65536], P('users'), may hold values from 0 to 1
- hist_len: int32 [64, 2], P('users'), may hold values from 64 to 512, as said below
- k_cache: bfloat16 [128, 512, 1024], P('users', None, 'mp'), may hold values from -6 to 6
- v_cache: bfloat16 [128, 512, 1024], P('users', None, 'mp'), may hold values from -6 to 6
- in_gain: float32 [1024], replicated, may hold values from 0.25 to 1.75
- w_uvqk: bfloat16 [1024, 4, 1024], P(None, None, 'mp'), may hold values from -0.1875 to 0.1875
- attn_gain: float32 [1024], P('mp'), may hold values from 0.25 to 1.75
- w_out: bfloat16 [1024, 1024], P(None, 'mp'), may hold values from -0.1875 to 0.1875
Outputs:
- scored: bfloat16 [65536, 1024], P('users', 'mp')
The draws below stay inside these ranges and needn't reach their ends.
Inputs may be any that keep to these rules, and one draw needn't show every extreme that they name: `cand_dest`: among the rows of one index of users, no owner is named by more than 32 rows, a bound that some block reaches. `hist_len`: for each owner, one of its 2 lengths is exactly 512.
All inputs are finite; a program needn't handle non-finite values.
Results may differ from the reference program's by a relative error of at most 0.0058.
Values may be sent and summed in bfloat16 or wider, within the bound.
A program may use at most 128 MiB of HBM per device.

```python
import math
import jax
import jax.numpy as jnp
import numpy as np
from jax import lax

D = 1024
HEADS = 8
HD = 128
UPD = 2
HLEN = 512
CAND_DEV = 1024
CAP = 32
USERS = 128
CANDS = 65536
N_USERS = 64


def draw_hist_len(key, part):
    key = jax.random.fold_in(key, 7)
    key_a = jax.random.fold_in(key, 1)
    key_b = jax.random.fold_in(key, 2)
    others = jax.random.randint(key_a, (N_USERS, UPD), HLEN // 8, HLEN + 1, dtype=jnp.int32)
    chosen = jax.random.randint(key_b, (N_USERS,), 0, UPD, dtype=jnp.int32)
    marked = jnp.arange(UPD, dtype=jnp.int32)[None, :] == chosen[:, None]
    return jnp.where(marked, jnp.int32(HLEN), others).astype(jnp.int32)


def with_ends(drawn, rng, low, top_value):
    extent = drawn.shape
    index_at = [jax.random.randint(jax.random.fold_in(rng, axis), (), 0, extent[axis]) for axis in range(len(extent))]
    drawn = drawn.at[tuple(index_at)].set(low)
    longest = extent.index(max(extent))
    index_at[longest] = (index_at[longest] + 1) % extent[longest]
    return drawn.at[tuple(index_at)].set(top_value)


def steps_of(key, extent, pieces, low, largest):
    def one(dim, blocks):
        heights = jax.random.uniform(jax.random.fold_in(jax.random.fold_in(key, 6), dim), (blocks,), jnp.float32, low / len(pieces), largest / len(pieces))
        return jnp.repeat(jnp.exp(heights), extent[dim] // blocks).reshape((-1,) + (1,) * (len(extent) - dim - 1))

    level = one(*pieces[0])
    for cut in pieces[1:]:
        level = level * one(*cut)
    return level


def shared_out(key, own, number, rows, count, top, limit, skew):
    order = jax.random.permutation(key, count)
    packed, ordinary = load_shares(count, rows * top, limit, skew, True), load_shares(count, rows * top, limit, skew, False)
    places = jnp.arange(count)

    def named(lengths, offset_by):
        used = int((lengths > 0).sum())
        fixed = max(1, used // 4)
        shifted = fixed + (places - fixed + offset_by * (used - fixed)) % max(1, count - fixed)
        return jnp.zeros((count,), jnp.int32).at[order[jnp.where(places < fixed, places, shifted)]].set(jnp.asarray(lengths, jnp.int32))

    lengths = jnp.where(number % 4 == 0, named(packed, number // 4), named(ordinary, number - number // 4 - 1))
    mixed = jax.random.permutation(jax.random.fold_in(own, 3), count)
    source_of, sink = mixed[0:count // 2 * 2:2], mixed[1:count // 2 * 2:2]
    margin = jnp.minimum(lengths[source_of] - 1, limit - lengths[sink]) // 2
    margin = jnp.where((source_of == order[0]) | (sink == order[0]) | (lengths[sink] == 0), 0, jnp.maximum(margin, 0))
    shifted = jax.random.randint(jax.random.fold_in(own, 4), (count // 2,), 0, 1 << 20) % (margin + 1)
    lengths = lengths.at[source_of].add(-shifted).at[sink].add(shifted)
    labels = jnp.searchsorted(jnp.cumsum(lengths), jnp.arange(rows * top), side="right").astype(jnp.int32)
    listing = labels.reshape(top, rows).T
    listing = listing[jax.random.permutation(jax.random.fold_in(own, 1), rows)]
    offset_by = jax.random.randint(jax.random.fold_in(own, 2), (rows, 1), 0, top)
    return jnp.take_along_axis(listing, (jnp.arange(top)[None, :] + offset_by) % top, axis=1)


def load_shares(count, total, bound, slope, full):
    weights = [(1 << 20) // math.isqrt(standing ** slope) + 1 for standing in range(1, count + 1)]
    largest = bound if full else min(bound, max(-(-total // count), total * weights[0] // sum(weights)))
    least = 1 if total - largest >= count - 1 else 0
    given, surplus = [largest] + [least] * (count - 1), total - largest - least * (count - 1)
    while surplus > 0:
        movable = [i for i in range(1, count) if given[i] < largest] or [i for i in range(1, count) if given[i] < bound]
        pool, left = sum([weights[i] for i in movable]), surplus
        for i in movable:
            addition = min(bound - given[i], max(1, left * weights[i] // pool), surplus)
            given[i] = given[i] + addition
            surplus = surplus - addition
    return np.array(given)


def normal_values(key, extent, scale, reach, shards=(), held_as=jnp.bfloat16):
    result = scale * jax.random.normal(key, extent, jnp.float32)
    if shards:
        result = result * steps_of(key, extent, shards, -0.22, 0.18)
    return jnp.clip(result, -reach, reach).astype(held_as)


def setup_inputs(seed: int = 0) -> dict:
    seeds = jax.random.split(jax.random.key(seed), 11)
    candidates = normal_values(seeds[0], (CANDS, D), 1.0, 6.0, ((0, 64), (1, 2)))
    cand_dest_keys = jax.random.split(jax.random.fold_in(seeds[1], 1), CANDS // CAND_DEV)
    cand_dest_turns = jax.random.permutation(jax.random.fold_in(seeds[1], 3), CANDS // CAND_DEV)
    cand_dest = jax.vmap(lambda own, number: shared_out(jax.random.fold_in(seeds[1], 2), own, number, CAND_DEV, N_USERS, 1, CAP, 2))(cand_dest_keys, cand_dest_turns).reshape((CANDS, 1))
    cand_slot = with_ends(jax.random.randint(seeds[2], (CANDS,), 0, UPD), jax.random.fold_in(seeds[2], 1), 0, UPD - 1).astype(jnp.int32)
    hist_len = draw_hist_len(jax.random.fold_in(seeds[10], 71), 0)
    k_cache = normal_values(seeds[4], (USERS, HLEN, D), 1.0, 6.0, ((0, 64), (2, 2)))
    v_cache = normal_values(seeds[5], (USERS, HLEN, D), 1.0, 6.0, ((0, 64), (2, 2)))
    in_gain = jnp.clip(1.0 + 0.15 * jax.random.normal(seeds[6], (D,), jnp.float32), 0.25, 1.75)
    w_uvqk = normal_values(seeds[7], (D, 4, D), D ** -0.5, 0.1875, ((2, 2),))
    attn_gain = jnp.clip(1.0 + 0.15 * jax.random.normal(seeds[8], (D,), jnp.float32), 0.25, 1.75)
    w_out = normal_values(seeds[9], (D, D), D ** -0.5, 0.1875, ((1, 2),))
    return {"candidates": candidates, "cand_dest": cand_dest, "cand_slot": cand_slot, "hist_len": hist_len, "k_cache": k_cache, "v_cache": v_cache, "in_gain": in_gain, "w_uvqk": w_uvqk, "attn_gain": attn_gain, "w_out": w_out}


def layer_norm(x, gain):
    mean = lax.optimization_barrier(jnp.mean(x, axis=-1, keepdims=True))
    var = lax.optimization_barrier(jnp.mean((x - mean) * (x - mean), axis=-1, keepdims=True))
    return (x - mean) * lax.rsqrt(var + 1e-05) * gain

def reference(candidates, cand_dest, cand_slot, hist_len, k_cache, v_cache, in_gain, w_uvqk, attn_gain, w_out):
    users_of = (cand_dest[:, 0] * UPD + cand_slot).astype(jnp.int32)
    lens_of = hist_len.reshape(-1)[users_of].astype(jnp.int32)
    xin = candidates.astype(jnp.float32)
    h = layer_norm(xin, in_gain).astype(jnp.bfloat16)
    proj = jnp.einsum('rd,dgc->rgc', h.astype(jnp.float32), w_uvqk.astype(jnp.float32))
    act = jax.nn.silu(proj).astype(jnp.bfloat16)
    scale = 1.0 / math.sqrt(HD)
    block = math.gcd(CANDS, 64)

    def one_block(index):
        start = (index * block).astype(jnp.int32)
        acts = lax.dynamic_slice_in_dim(act, start, block, 0)
        users_b = lax.dynamic_slice_in_dim(users_of, start, block, 0)
        lens_b = lax.dynamic_slice_in_dim(lens_of, start, block, 0)
        qq = acts[:, 2].reshape(block, HEADS, HD).astype(jnp.float32)
        kk = acts[:, 3].reshape(block, HEADS, HD).astype(jnp.float32)
        vv = acts[:, 1].reshape(block, HEADS, HD).astype(jnp.float32)
        keys = k_cache[users_b].reshape(block, HLEN, HEADS, HD).astype(jnp.float32)
        vals = v_cache[users_b].reshape(block, HLEN, HEADS, HD).astype(jnp.float32)
        scores = jnp.einsum('bhc,bphc->bhp', qq, keys) * scale
        valid = jnp.arange(HLEN)[None, None, :] < lens_b[:, None, None]
        wts = jnp.where(valid, jax.nn.silu(scores), 0.0).astype(jnp.bfloat16)
        summed = jnp.einsum('bhp,bphc->bhc', wts.astype(jnp.float32), vals)
        self_w = jax.nn.silu(jnp.einsum('bhc,bhc->bh', qq, kk) * scale).astype(jnp.bfloat16)
        summed = summed + self_w.astype(jnp.float32)[:, :, None] * vv
        denom = lens_b.astype(jnp.float32) + 1.0
        return (summed / denom[:, None, None]).reshape(block, D)
    attn = lax.map(one_block, jnp.arange(CANDS // block, dtype=jnp.int32)).reshape(CANDS, D)
    u_part = act[:, 0].astype(jnp.float32)
    y_rows = (layer_norm(attn, attn_gain) * u_part).astype(jnp.bfloat16)
    out = xin + jnp.dot(y_rows, w_out, preferred_element_type=jnp.float32)
    return out.astype(jnp.bfloat16)
```

```python
import functools
import math

import jax
import jax.numpy as jnp
from jax import lax
from jax.experimental import pallas as pl
from jax.experimental.pallas import tpu as pltpu
from jax.sharding import PartitionSpec as P

MESH = pl.DeviceIdType.MESH
D = 1024
W = 512
HD = 128
HEADS_HERE = W // HD
HLEN = 512
ROWS = 1024
PEERS = 64
SIDE = 4
CAP = 32
SLOTS = PEERS * CAP
GROUP = 8
GROUPS = PEERS // GROUP
GR = GROUP * CAP
STEP = 59
STEP_INV = 51
LAG = 4
EPS = 1e-05
SCALE = 1.0 / math.sqrt(HD)
F32 = jnp.float32
BF16 = jnp.bfloat16


def silu(x):
    t = 0.5 * x
    return t + t * jnp.tanh(t)


def digits(k):
    return k % SIDE, (k // SIDE) % SIDE, k // (SIDE * SIDE)


def ahead(me, j):
    x, y, z = digits(me)
    a, b, c = digits((j * STEP) % PEERS)
    return ((z + c) % SIDE) * SIDE * SIDE + ((y + b) % SIDE) * SIDE + (x + a) % SIDE


def behind(me, j):
    x, y, z = digits(me)
    a, b, c = digits((j * STEP) % PEERS)
    return (
        ((z + SIDE - c) % SIDE) * SIDE * SIDE
        + ((y + SIDE - b) % SIDE) * SIDE
        + (x + SIDE - a) % SIDE
    )


def mirrored(j):
    a, b, c = digits((j * STEP) % PEERS)
    k = ((SIDE - c) % SIDE) * SIDE * SIDE + ((SIDE - b) % SIDE) * SIDE + (SIDE - a) % SIDE
    return (k * STEP_INV) % PEERS


def kernel(
    x_hbm, dest_ref, slot_ref, hist_ref, k_hbm, v_hbm, in_gain_ref, w_hbm, attn_gain_ref, wout_hbm,
    out_ref,
    x_v, w_v, wout_v, k_v, v_v, v01, fs_row, fs_col, meta, metar, mask_in, inv_len, gain_v,
    xs_own, xs_peer, h_v, q_send, q_recv, a_send, back, u_v, self_v, st_send, st_recv,
    y_own, y_peer, acc,
    load_sem, x_ssem, x_rsem, q_ssem, q_rsem, a_ssem, a_rsem, m_ssem, m_rsem, s_ssem, s_rsem,
    y_ssem, y_rsem,
):
    me = lax.axis_index("users")
    mp = lax.axis_index("mp")
    other = 1 - mp
    own_at = pl.multiple_of(mp * W, W)
    peer_at = pl.multiple_of(other * W, W)

    loads = [
        pltpu.make_async_copy(x_hbm, x_v, load_sem.at[0]),
        pltpu.make_async_copy(w_hbm.at[2, pl.ds(own_at, W)], w_v.at[2, pl.ds(0, W)], load_sem.at[1]),
        pltpu.make_async_copy(w_hbm.at[2, pl.ds(peer_at, W)], w_v.at[2, pl.ds(W, W)], load_sem.at[2]),
        pltpu.make_async_copy(k_hbm, k_v, load_sem.at[3]),
        pltpu.make_async_copy(v_hbm, v_v, load_sem.at[4]),
    ]
    late = [
        pltpu.make_async_copy(wout_hbm.at[pl.ds(own_at, W)], wout_v.at[pl.ds(0, W)], load_sem.at[5]),
        pltpu.make_async_copy(wout_hbm.at[pl.ds(peer_at, W)], wout_v.at[pl.ds(W, W)], load_sem.at[6]),
    ]
    for n, g in enumerate((0, 1, 3)):
        late.append(
            pltpu.make_async_copy(
                w_hbm.at[g, pl.ds(own_at, W)], w_v.at[g, pl.ds(0, W)], load_sem.at[7 + 2 * n]
            )
        )
        late.append(
            pltpu.make_async_copy(
                w_hbm.at[g, pl.ds(peer_at, W)], w_v.at[g, pl.ds(W, W)], load_sem.at[8 + 2 * n]
            )
        )
    for c in loads + late:
        c.start()

    barrier = pltpu.get_barrier_semaphore()

    def greet(j, carry):
        pl.semaphore_signal(barrier, inc=1, device_id=(ahead(me, j), mp), device_id_type=MESH)
        return carry

    pl.semaphore_signal(barrier, inc=1, device_id=(me, other), device_id_type=MESH)
    lax.fori_loop(1, PEERS, greet, 0)

    dest = dest_ref[...]
    slot = slot_ref[...]
    mx, my, mz = digits(me)
    kx = ((dest & 3) + (SIDE - mx)) & 3
    ky = (((dest >> 2) & 3) + (SIDE - my)) & 3
    kz = ((dest >> 4) + (SIDE - mz)) & 3
    number = ((kx + 4 * ky + 16 * kz) * STEP_INV) & (PEERS - 1)
    key = 2 * number + slot
    hot = (lax.broadcasted_iota(jnp.int32, (2 * PEERS, ROWS), 0) == key).astype(F32)
    before = jnp.zeros((2 * PEERS, 256), F32)
    pos_parts = []
    tri = (
        lax.broadcasted_iota(jnp.int32, (256, 256), 0)
        < lax.broadcasted_iota(jnp.int32, (256, 256), 1)
    ).astype(F32).astype(BF16)
    count = jnp.zeros((2 * PEERS, 1), F32)
    for b in range(ROWS // 256):
        part = hot[:, b * 256 : (b + 1) * 256]
        before = jnp.dot(part.astype(BF16), tri, preferred_element_type=F32) + count
        pos_parts.append(jnp.sum(before * part, axis=0, keepdims=True))
        count = count + jnp.sum(part, axis=1, keepdims=True)
    pos = jnp.concatenate(pos_parts, axis=1)
    fs = (number * CAP).astype(F32) + jnp.where(slot == 0, pos, (CAP - 1) - pos)
    fs_row[...] = jnp.broadcast_to(fs, (8, ROWS))
    fs_col[...] = jnp.broadcast_to(fs, (HD, ROWS)).T
    same = lax.broadcasted_iota(jnp.int32, (PEERS, ROWS), 0) == number
    first = jnp.sum(jnp.where(same & (slot == 0), 1.0, 0.0), axis=1, keepdims=True)
    hist = hist_ref[...].astype(F32)
    len0, len1 = hist[:, 0:1], hist[:, 1:2]
    lane = lax.broadcasted_iota(jnp.int32, (PEERS, HD), 1)
    meta_rows = jnp.where(lane < 64, first, jnp.where(lane < 96, len0, len1))
    meta[...] = meta_rows.reshape(PEERS, 1, HD)
    metar[0] = meta[0]
    gain_v[...] = jnp.concatenate(
        [in_gain_ref[pl.ds(mp, 1), :], in_gain_ref[pl.ds(other, 1), :]], axis=1
    )
    acc[...] = jnp.zeros_like(acc)

    def rows_of(g):
        return pl.ds(pl.multiple_of(g * GR, GR), GR)

    def chunk_of(j):
        return pl.ds(pl.multiple_of(j * CAP, CAP), CAP)

    def x_copy(g):
        return pltpu.make_async_remote_copy(
            src_ref=xs_own.at[rows_of(g)], dst_ref=xs_peer.at[rows_of(g)],
            send_sem=x_ssem.at[g], recv_sem=x_rsem.at[g],
            device_id=(me, other), device_id_type=MESH,
        )

    def q_copy(g, j):
        return pltpu.make_async_remote_copy(
            src_ref=q_send.at[chunk_of(j)], dst_ref=q_recv.at[chunk_of(j)],
            send_sem=q_ssem.at[g], recv_sem=q_rsem.at[g],
            device_id=(ahead(me, j), mp), device_id_type=MESH,
        )

    def a_copy(g, j):
        return pltpu.make_async_remote_copy(
            src_ref=a_send.at[chunk_of(j)], dst_ref=back.at[chunk_of(j)],
            send_sem=a_ssem.at[g], recv_sem=a_rsem.at[g],
            device_id=(behind(me, j), mp), device_id_type=MESH,
        )

    def s_copy(g):
        return pltpu.make_async_remote_copy(
            src_ref=st_send.at[rows_of(g)], dst_ref=st_recv.at[rows_of(g)],
            send_sem=s_ssem.at[g], recv_sem=s_rsem.at[g],
            device_id=(me, other), device_id_type=MESH,
        )

    def y_copy(g):
        return pltpu.make_async_remote_copy(
            src_ref=y_own.at[rows_of(g)], dst_ref=y_peer.at[rows_of(g)],
            send_sem=y_ssem.at[g], recv_sem=y_rsem.at[g],
            device_id=(me, other), device_id_type=MESH,
        )

    def m_copy(j):
        return pltpu.make_async_remote_copy(
            src_ref=meta.at[j], dst_ref=metar.at[j],
            send_sem=m_ssem.at[0], recv_sem=m_rsem.at[0],
            device_id=(ahead(me, j), mp), device_id_type=MESH,
        )

    def gather(g):
        slots = lax.broadcasted_iota(jnp.int32, (GR, ROWS), 0).astype(F32) + (g * GR).astype(F32)
        pick = jnp.where(slots == fs_row[0:1, :], 1.0, 0.0).astype(BF16)
        xs_own[rows_of(g), :] = jnp.dot(pick, x_v[...], preferred_element_type=F32).astype(BF16)
        x_copy(g).start()

    def norm_and_query(g):
        x_copy(g).wait_recv()
        xo = xs_own[rows_of(g), :].astype(F32)
        xp = xs_peer[rows_of(g), :].astype(F32)
        xf = jnp.concatenate([xo, xp], axis=1)
        mean = jnp.sum(xf, axis=1, keepdims=True) * (1.0 / D)
        c = xf - mean
        var = jnp.sum(c * c, axis=1, keepdims=True) * (1.0 / D)
        h = (c * lax.rsqrt(var + EPS) * gain_v[...]).astype(BF16)
        h_v[rows_of(g), :] = h
        q_send[rows_of(g), :] = silu(jnp.dot(h, w_v[2], preferred_element_type=F32)).astype(BF16)

    def send_queries(g):
        lo = jnp.where(g == 0, 1, g * GROUP)

        def one(j, carry):
            q_copy(g, j).start()
            return carry

        lax.fori_loop(lo, (g + 1) * GROUP, one, 0)

    def project_rest(g):
        h = h_v[rows_of(g), :]
        u_v[rows_of(g), :] = silu(jnp.dot(h, w_v[0], preferred_element_type=F32)).astype(BF16)
        v = silu(jnp.dot(h, w_v[1], preferred_element_type=F32)).astype(BF16).astype(F32)
        k = silu(jnp.dot(h, w_v[3], preferred_element_type=F32)).astype(BF16).astype(F32)
        q = q_send[rows_of(g), :].astype(F32)
        qk = q * k
        for n in range(HEADS_HERE):
            cols = slice(n * HD, (n + 1) * HD)
            s = jnp.sum(qk[:, cols], axis=1, keepdims=True) * SCALE
            sw = silu(s).astype(BF16).astype(F32)
            self_v[rows_of(g), cols] = sw * v[:, cols] * inv_len[rows_of(g), :]

    def attend(g):
        m1 = mask_in[rows_of(g), :]
        m0 = 1.0 - m1
        rs = m0 * (1.0 / (len0 + 1.0)) + m1 * (1.0 / (len1 + 1.0))
        for n in range(HEADS_HERE):
            cols = slice(n * HD, (n + 1) * HD)
            qf = q_recv[rows_of(g), cols].astype(F32)
            q01 = jnp.concatenate([(qf * m0).astype(BF16), (qf * m1).astype(BF16)], axis=1)
            k01 = jnp.concatenate([k_v[0, :, cols], k_v[1, :, cols]], axis=1)
            s = lax.dot_general(q01, k01, (((1,), (1,)), ((), ())), preferred_element_type=F32)
            t = s * (0.5 * SCALE)
            wts = (t + t * jnp.tanh(t)).astype(BF16)
            o = jnp.dot(wts, v01[n], preferred_element_type=F32)
            a = (o[:, :HD] * m0 + o[:, HD:] * m1) * rs
            a_send[rows_of(g), cols] = a.astype(BF16)

    def send_back(g):
        lo = jnp.where(g == 0, 1, g * GROUP)

        def one(j, carry):
            a_copy(g, j).start()
            return carry

        lax.fori_loop(lo, (g + 1) * GROUP, one, 0)

    def finish_sums(g):
        a = back[rows_of(g), :].astype(F32) + self_v[rows_of(g), :]
        mean = jnp.sum(a, axis=1, keepdims=True) * (1.0 / W)
        c = a - mean
        m2 = jnp.sum(c * c, axis=1, keepdims=True)
        self_v[rows_of(g), :] = a
        lanes = lax.broadcasted_iota(jnp.int32, (GR, HD), 1)
        st_send[rows_of(g), :] = jnp.where(lanes < 64, mean, m2)
        s_copy(g).start()

    def normalize(g):
        s_copy(g).wait_recv()
        so = st_send[rows_of(g), :]
        sp = st_recv[rows_of(g), :]
        mo, mp_ = so[:, 0:1], sp[:, 0:1]
        mean = 0.5 * (mo + mp_)
        gap = mo - mp_
        var = (so[:, 64:65] + sp[:, 64:65] + (0.5 * W) * gap * gap) * (1.0 / D)
        y = (
            (self_v[rows_of(g), :] - mean)
            * lax.rsqrt(var + EPS)
            * attn_gain_ref[...]
            * u_v[rows_of(g), :].astype(F32)
        )
        y_own[rows_of(g), :] = y.astype(BF16)
        y_copy(g).start()

    def output(g):
        y_copy(g).wait_recv()
        y = jnp.concatenate([y_own[rows_of(g), :], y_peer[rows_of(g), :]], axis=1)
        p = jnp.dot(y, wout_v[...], preferred_element_type=F32)
        fin = (xs_own[rows_of(g), :].astype(F32) + p).astype(BF16)
        base = (g * GR).astype(F32)
        lanes = lax.broadcasted_iota(jnp.int32, (ROWS, HD), 1).astype(F32) + base
        f = fs_col[...]
        pick = jnp.concatenate(
            [jnp.where(f == lanes + float(n * HD), 1.0, 0.0).astype(BF16) for n in range(GR // HD)],
            axis=1,
        )
        acc[...] += jnp.dot(pick, fin, preferred_element_type=F32)

    pl.semaphore_wait(barrier, PEERS)

    def send_meta(j, carry):
        m_copy(j).start()
        return carry

    lax.fori_loop(1, PEERS, send_meta, 0)
    for c in loads[:3]:
        c.wait()

    def head(i, carry):
        @pl.when(i < GROUPS)
        def _():
            gather(i)

        @pl.when(i >= 1)
        def _():
            norm_and_query(i - 1)

            @pl.when(i == 1)
            def _():
                q_recv[pl.ds(0, CAP), :] = q_send[pl.ds(0, CAP), :]

            send_queries(i - 1)

        return carry

    lax.fori_loop(0, GROUPS + 1, head, 0)

    for c in loads[3:] + late:
        c.wait()
    place = lax.broadcasted_iota(jnp.int32, (HLEN, W), 0).astype(F32)
    for user, length in ((0, len0), (1, len1)):
        kept = jnp.where(place < length, v_v[user].astype(F32), 0.0).astype(BF16)
        for n in range(HEADS_HERE):
            v01[n, :, user * HD : (user + 1) * HD] = kept[:, n * HD : (n + 1) * HD]

    pltpu.make_async_copy(
        metar.at[pl.ds(1, PEERS - 1)], metar.at[pl.ds(1, PEERS - 1)], m_rsem.at[0]
    ).wait()
    in_chunk = lax.broadcasted_iota(jnp.int32, (CAP, HD), 0).astype(F32)

    def masks(j, carry):
        mask_in[chunk_of(j), :] = jnp.where(in_chunk >= metar[j][:, 0:1], 1.0, 0.0)
        theirs = metar[mirrored(j)]
        l0, l1 = theirs[:, 64:65], theirs[:, 96:97]
        length = jnp.where(in_chunk >= meta[j][:, 0:1], l1, l0)
        inv_len[chunk_of(j), :] = 1.0 / (length + 1.0)
        return carry

    lax.fori_loop(0, PEERS, masks, 0)

    def wait_group(buf, sem, g):
        @pl.when(g == 0)
        def _():
            rows = pl.ds(CAP, GR - CAP)
            pltpu.make_async_copy(buf.at[rows], buf.at[rows], sem.at[0]).wait()

        @pl.when(g > 0)
        def _():
            pltpu.make_async_copy(buf.at[rows_of(g)], buf.at[rows_of(g)], sem.at[g]).wait()

    def body(i, carry):
        @pl.when(i < GROUPS)
        def _():
            project_rest(i)
            wait_group(q_recv, q_rsem, i)
            attend(i)

            @pl.when(i == 0)
            def _():
                back[pl.ds(0, CAP), :] = a_send[pl.ds(0, CAP), :]

            send_back(i)

        @pl.when(jnp.logical_and(i >= LAG, i < GROUPS + LAG))
        def _():
            wait_group(back, a_rsem, i - LAG)
            finish_sums(i - LAG)

        @pl.when(jnp.logical_and(i >= LAG + 1, i < GROUPS + LAG + 1))
        def _():
            normalize(i - LAG - 1)

        @pl.when(i >= LAG + 2)
        def _():
            output(i - LAG - 2)

        return carry

    lax.fori_loop(0, GROUPS + LAG + 2, body, 0)
    out_ref[...] = acc[...].astype(BF16)

    def drain(g, carry):
        x_copy(g).wait_send()
        s_copy(g).wait_send()
        y_copy(g).wait_send()
        wait_group(q_send, q_ssem, g)
        wait_group(a_send, a_ssem, g)
        return carry

    lax.fori_loop(0, GROUPS, drain, 0)
    pltpu.make_async_copy(
        meta.at[pl.ds(1, PEERS - 1)], meta.at[pl.ds(1, PEERS - 1)], m_ssem.at[0]
    ).wait()


def body(
    candidates, cand_dest, cand_slot, hist_len, k_cache, v_cache, in_gain, w_uvqk, attn_gain, w_out
):
    vmem = pl.BlockSpec(memory_space=pltpu.VMEM)
    hbm = pl.BlockSpec(memory_space=pl.ANY)
    dma = pltpu.SemaphoreType.DMA
    return pl.pallas_call(
        kernel,
        out_shape=jax.ShapeDtypeStruct((ROWS, W), BF16),
        in_specs=[hbm, vmem, vmem, vmem, hbm, hbm, vmem, hbm, vmem, hbm],
        out_specs=vmem,
        scratch_shapes=[
            pltpu.VMEM((ROWS, W), BF16),
            pltpu.VMEM((4, D, W), BF16),
            pltpu.VMEM((D, W), BF16),
            pltpu.VMEM((2, HLEN, W), BF16),
            pltpu.VMEM((2, HLEN, W), BF16),
            pltpu.VMEM((HEADS_HERE, HLEN, 2 * HD), BF16),
            pltpu.VMEM((8, ROWS), F32),
            pltpu.VMEM((ROWS, HD), F32),
            pltpu.VMEM((PEERS, 1, HD), F32),
            pltpu.VMEM((PEERS, 1, HD), F32),
            pltpu.VMEM((SLOTS, HD), F32),
            pltpu.VMEM((SLOTS, HD), F32),
            pltpu.VMEM((1, D), F32),
            pltpu.VMEM((SLOTS, W), BF16),
            pltpu.VMEM((SLOTS, W), BF16),
            pltpu.VMEM((SLOTS, D), BF16),
            pltpu.VMEM((SLOTS, W), BF16),
            pltpu.VMEM((SLOTS, W), BF16),
            pltpu.VMEM((SLOTS, W), BF16),
            pltpu.VMEM((SLOTS, W), BF16),
            pltpu.VMEM((SLOTS, W), BF16),
            pltpu.VMEM((SLOTS, W), F32),
            pltpu.VMEM((SLOTS, HD), F32),
            pltpu.VMEM((SLOTS, HD), F32),
            pltpu.VMEM((SLOTS, W), BF16),
            pltpu.VMEM((SLOTS, W), BF16),
            pltpu.VMEM((ROWS, W), F32),
            dma((13,)),
            dma((GROUPS,)), dma((GROUPS,)),
            dma((GROUPS,)), dma((GROUPS,)),
            dma((GROUPS,)), dma((GROUPS,)),
            dma((1,)), dma((1,)),
            dma((GROUPS,)), dma((GROUPS,)),
            dma((GROUPS,)), dma((GROUPS,)),
        ],
        compiler_params=pltpu.CompilerParams(
            collective_id=0, has_side_effects=True, vmem_limit_bytes=60 * 2**20
        ),
        cost_estimate=pl.CostEstimate(
            flops=20 * 10**9, bytes_accessed=10 * 10**6, transcendentals=9 * 10**6
        ),
        name="routed_ranking",
    )(
        candidates,
        cand_dest.reshape(1, ROWS),
        cand_slot.reshape(1, ROWS),
        hist_len,
        k_cache,
        v_cache,
        in_gain.reshape(2, W),
        w_uvqk.transpose(1, 0, 2),
        attn_gain.reshape(1, W),
        w_out,
    )


def solution(mesh):
    return jax.shard_map(
        body,
        mesh=mesh,
        in_specs=(
            P("users", "mp"),
            P("users", None),
            P("users"),
            P("users", None),
            P("users", None, "mp"),
            P("users", None, "mp"),
            P(),
            P(None, None, "mp"),
            P("mp"),
            P(None, "mp"),
        ),
        out_specs=P("users", "mp"),
        check_vma=False,
    )
```

```python
import functools
import math

import jax
import jax.numpy as jnp
from jax import lax
from jax.experimental import pallas as pl
from jax.experimental.pallas import tpu as pltpu
from jax.sharding import PartitionSpec as P

MESH = pl.DeviceIdType.MESH
D = 1024
W = 512
HD = 128
HEADS_HERE = W // HD
HLEN = 512
ROWS = 1024
PEERS = 64
SIDE = 4
CAP = 32
SLOTS = PEERS * CAP
GROUP = 8
GROUPS = PEERS // GROUP
GR = GROUP * CAP
STEP = 59
STEP_INV = 51
LAG = 4
EPS = 1e-05
VMEM_LIMIT = 54 * 2**20
ABL = CAP
SCALE = 1.0 / math.sqrt(HD)
F32 = jnp.float32
BF16 = jnp.bfloat16


def silu(x):
    t = 0.5 * x
    return t + t * jnp.tanh(t)


def digits(k):
    return k % SIDE, (k // SIDE) % SIDE, k // (SIDE * SIDE)


def ahead(me, j):
    x, y, z = digits(me)
    a, b, c = digits((j * STEP) % PEERS)
    return ((z + c) % SIDE) * SIDE * SIDE + ((y + b) % SIDE) * SIDE + (x + a) % SIDE


def behind(me, j):
    x, y, z = digits(me)
    a, b, c = digits((j * STEP) % PEERS)
    return (
        ((z + SIDE - c) % SIDE) * SIDE * SIDE
        + ((y + SIDE - b) % SIDE) * SIDE
        + (x + SIDE - a) % SIDE
    )


def mirrored(j):
    a, b, c = digits((j * STEP) % PEERS)
    k = ((SIDE - c) % SIDE) * SIDE * SIDE + ((SIDE - b) % SIDE) * SIDE + (SIDE - a) % SIDE
    return (k * STEP_INV) % PEERS


def kernel(
    x_hbm, dest_ref, slot_ref, hist_ref, k_hbm, v_hbm, in_gain_ref, w_hbm, attn_gain_ref, wout_hbm,
    out_ref,
    x_v, w_raw, w_v, wout_v, k_v, v_v, v01, fs_row, fs_col, meta, metar, mask_in, inv_len, gain_v,
    xs_own, xs_peer, h_v, q_send, q_recv, a_send, back, u_v, self_v, st_send, st_recv,
    y_own, y_peer, acc,
    load_sem, x_ssem, x_rsem, q_ssem, q_rsem, a_ssem, a_rsem, m_ssem, m_rsem, s_ssem, s_rsem,
    y_ssem, y_rsem,
):
    me = lax.axis_index("users")
    mp = lax.axis_index("mp")
    other = 1 - mp
    own_at = pl.multiple_of(mp * W, W)
    peer_at = pl.multiple_of(other * W, W)

    barrier = pltpu.get_barrier_semaphore()

    def greet(j, carry):
        pl.semaphore_signal(barrier, inc=1, device_id=(ahead(me, j), mp), device_id_type=MESH)
        return carry

    pl.semaphore_signal(barrier, inc=1, device_id=(me, other), device_id_type=MESH)
    lax.fori_loop(1, PEERS, greet, 0)

    loads = [
        pltpu.make_async_copy(x_hbm, x_v, load_sem.at[0]),
        pltpu.make_async_copy(w_hbm, w_raw, load_sem.at[1]),
        pltpu.make_async_copy(wout_hbm.at[pl.ds(own_at, W)], wout_v.at[pl.ds(0, W)], load_sem.at[2]),
        pltpu.make_async_copy(k_hbm, k_v, load_sem.at[3]),
        pltpu.make_async_copy(v_hbm, v_v, load_sem.at[4]),
    ]
    loads.append(
        pltpu.make_async_copy(wout_hbm.at[pl.ds(peer_at, W)], wout_v.at[pl.ds(W, W)], load_sem.at[5])
    )
    for c in loads:
        c.start()

    dest = dest_ref[...]
    slot = slot_ref[...]
    mx, my, mz = digits(me)
    kx = ((dest & 3) + (SIDE - mx)) & 3
    ky = (((dest >> 2) & 3) + (SIDE - my)) & 3
    kz = ((dest >> 4) + (SIDE - mz)) & 3
    number = ((kx + 4 * ky + 16 * kz) * STEP_INV) & (PEERS - 1)
    key = 2 * number + slot
    hot = (lax.broadcasted_iota(jnp.int32, (2 * PEERS, ROWS), 0) == key).astype(F32)
    before = jnp.zeros((2 * PEERS, 256), F32)
    pos_parts = []
    tri = (
        lax.broadcasted_iota(jnp.int32, (256, 256), 0)
        < lax.broadcasted_iota(jnp.int32, (256, 256), 1)
    ).astype(F32).astype(BF16)
    count = jnp.zeros((2 * PEERS, 1), F32)
    for b in range(ROWS // 256):
        part = hot[:, b * 256 : (b + 1) * 256]
        before = jnp.dot(part.astype(BF16), tri, preferred_element_type=F32) + count
        pos_parts.append(jnp.sum(before * part, axis=0, keepdims=True))
        count = count + jnp.sum(part, axis=1, keepdims=True)
    pos = jnp.concatenate(pos_parts, axis=1)
    fs = (number * CAP).astype(F32) + jnp.where(slot == 0, pos, (CAP - 1) - pos)
    fs_row[...] = jnp.broadcast_to(fs, (8, ROWS))
    fs_col[...] = jnp.broadcast_to(fs, (HD, ROWS)).T
    same = lax.broadcasted_iota(jnp.int32, (PEERS, ROWS), 0) == number
    first = jnp.sum(jnp.where(same & (slot == 0), 1.0, 0.0), axis=1, keepdims=True)
    hist = hist_ref[...].astype(F32)
    len0, len1 = hist[:, 0:1], hist[:, 1:2]
    lane = lax.broadcasted_iota(jnp.int32, (PEERS, HD), 1)
    meta_rows = jnp.where(lane < 64, first, jnp.where(lane < 96, len0, len1))
    meta[...] = meta_rows.reshape(PEERS, 1, HD)
    metar[0] = meta[0]
    gain_v[...] = jnp.concatenate(
        [in_gain_ref[:, pl.ds(own_at, W)], in_gain_ref[:, pl.ds(peer_at, W)]], axis=1
    )
    acc[...] = jnp.zeros_like(acc)

    def rows_of(g):
        return pl.ds(pl.multiple_of(g * GR, GR), GR)

    def chunk_of(j):
        return pl.ds(pl.multiple_of(j * CAP, CAP), CAP)

    def abl_of(j):
        return pl.ds(pl.multiple_of(j * CAP, CAP), ABL)

    def x_copy(g):
        return pltpu.make_async_remote_copy(
            src_ref=xs_own.at[rows_of(g)], dst_ref=xs_peer.at[rows_of(g)],
            send_sem=x_ssem.at[g], recv_sem=x_rsem.at[g],
            device_id=(me, other), device_id_type=MESH,
        )

    def q_copy(g, j):
        return pltpu.make_async_remote_copy(
            src_ref=q_send.at[abl_of(j)], dst_ref=q_recv.at[abl_of(j)],
            send_sem=q_ssem.at[g], recv_sem=q_rsem.at[g],
            device_id=(ahead(me, j), mp), device_id_type=MESH,
        )

    def a_copy(g, j):
        return pltpu.make_async_remote_copy(
            src_ref=a_send.at[abl_of(j)], dst_ref=back.at[abl_of(j)],
            send_sem=a_ssem.at[g], recv_sem=a_rsem.at[g],
            device_id=(behind(me, j), mp), device_id_type=MESH,
        )

    def s_copy(g):
        return pltpu.make_async_remote_copy(
            src_ref=st_send.at[rows_of(g)], dst_ref=st_recv.at[rows_of(g)],
            send_sem=s_ssem.at[g], recv_sem=s_rsem.at[g],
            device_id=(me, other), device_id_type=MESH,
        )

    def y_copy(g):
        return pltpu.make_async_remote_copy(
            src_ref=y_own.at[rows_of(g)], dst_ref=y_peer.at[rows_of(g)],
            send_sem=y_ssem.at[g], recv_sem=y_rsem.at[g],
            device_id=(me, other), device_id_type=MESH,
        )

    def m_copy(j):
        return pltpu.make_async_remote_copy(
            src_ref=meta.at[j], dst_ref=metar.at[j],
            send_sem=m_ssem.at[0], recv_sem=m_rsem.at[0],
            device_id=(ahead(me, j), mp), device_id_type=MESH,
        )

    def gather(g):
        slots = lax.broadcasted_iota(jnp.int32, (GR, ROWS), 0).astype(F32) + (g * GR).astype(F32)
        pick = jnp.where(slots == fs_row[0:1, :], 1.0, 0.0).astype(BF16)
        xs_own[rows_of(g), :] = jnp.dot(pick, x_v[...], preferred_element_type=F32).astype(BF16)
        x_copy(g).start()

    def norm_and_query(g):
        x_copy(g).wait_recv()
        xo = xs_own[rows_of(g), :].astype(F32)
        xp = xs_peer[rows_of(g), :].astype(F32)
        xf = jnp.concatenate([xo, xp], axis=1)
        mean = jnp.sum(xf, axis=1, keepdims=True) * (1.0 / D)
        c = xf - mean
        var = jnp.sum(c * c, axis=1, keepdims=True) * (1.0 / D)
        h = (c * lax.rsqrt(var + EPS) * gain_v[...]).astype(BF16)
        h_v[rows_of(g), :] = h
        q_send[rows_of(g), :] = silu(jnp.dot(h, w_v[2], preferred_element_type=F32)).astype(BF16)

    def send_queries(g):
        lo = jnp.where(g == 0, 1, g * GROUP)

        def one(j, carry):
            q_copy(g, j).start()
            return carry

        lax.fori_loop(lo, (g + 1) * GROUP, one, 0)

    def project_rest(g):
        h = h_v[rows_of(g), :]
        u_v[rows_of(g), :] = silu(jnp.dot(h, w_v[0], preferred_element_type=F32)).astype(BF16)
        v = silu(jnp.dot(h, w_v[1], preferred_element_type=F32)).astype(BF16).astype(F32)
        k = silu(jnp.dot(h, w_v[3], preferred_element_type=F32)).astype(BF16).astype(F32)
        q = q_send[rows_of(g), :].astype(F32)
        qk = q * k
        for n in range(HEADS_HERE):
            cols = slice(n * HD, (n + 1) * HD)
            s = jnp.sum(qk[:, cols], axis=1, keepdims=True) * SCALE
            sw = silu(s).astype(BF16).astype(F32)
            self_v[rows_of(g), cols] = sw * v[:, cols] * inv_len[rows_of(g), :]

    def attend(g):
        m1 = mask_in[rows_of(g), :]
        m0 = 1.0 - m1
        rs = m0 * (1.0 / (len0 + 1.0)) + m1 * (1.0 / (len1 + 1.0))
        for n in range(HEADS_HERE):
            cols = slice(n * HD, (n + 1) * HD)
            qf = q_recv[rows_of(g), cols].astype(F32)
            q01 = jnp.concatenate([(qf * m0).astype(BF16), (qf * m1).astype(BF16)], axis=1)
            k01 = jnp.concatenate([k_v[0, :, cols], k_v[1, :, cols]], axis=1)
            s = lax.dot_general(q01, k01, (((1,), (1,)), ((), ())), preferred_element_type=F32)
            t = s * (0.5 * SCALE)
            wts = (t + t * jnp.tanh(t)).astype(BF16)
            o = jnp.dot(wts, v01[n], preferred_element_type=F32)
            a = (o[:, :HD] * m0 + o[:, HD:] * m1) * rs
            a_send[rows_of(g), cols] = a.astype(BF16)

    def send_back(g):
        lo = jnp.where(g == 0, 1, g * GROUP)

        def one(j, carry):
            a_copy(g, j).start()
            return carry

        lax.fori_loop(lo, (g + 1) * GROUP, one, 0)

    def finish_sums(g):
        a = back[rows_of(g), :].astype(F32) + self_v[rows_of(g), :]
        mean = jnp.sum(a, axis=1, keepdims=True) * (1.0 / W)
        c = a - mean
        m2 = jnp.sum(c * c, axis=1, keepdims=True)
        self_v[rows_of(g), :] = a
        lanes = lax.broadcasted_iota(jnp.int32, (GR, HD), 1)
        st_send[rows_of(g), :] = jnp.where(lanes < 64, mean, m2)
        s_copy(g).start()

    def normalize(g):
        s_copy(g).wait_recv()
        so = st_send[rows_of(g), :]
        sp = st_recv[rows_of(g), :]
        mo, mp_ = so[:, 0:1], sp[:, 0:1]
        mean = 0.5 * (mo + mp_)
        gap = mo - mp_
        var = (so[:, 64:65] + sp[:, 64:65] + (0.5 * W) * gap * gap) * (1.0 / D)
        y = (
            (self_v[rows_of(g), :] - mean)
            * lax.rsqrt(var + EPS)
            * attn_gain_ref[...]
            * u_v[rows_of(g), :].astype(F32)
        )
        y_own[rows_of(g), :] = y.astype(BF16)
        y_copy(g).start()

    def output(g):
        y_copy(g).wait_recv()
        y = jnp.concatenate([y_own[rows_of(g), :], y_peer[rows_of(g), :]], axis=1)
        p = jnp.dot(y, wout_v[...], preferred_element_type=F32)
        fin = (xs_own[rows_of(g), :].astype(F32) + p).astype(BF16)
        base = (g * GR).astype(F32)
        lanes = lax.broadcasted_iota(jnp.int32, (ROWS, HD), 1).astype(F32) + base
        f = fs_col[...]
        pick = jnp.concatenate(
            [jnp.where(f == lanes + float(n * HD), 1.0, 0.0).astype(BF16) for n in range(GR // HD)],
            axis=1,
        )
        acc[...] += jnp.dot(pick, fin, preferred_element_type=F32)

    pl.semaphore_wait(barrier, PEERS)

    def send_meta(j, carry):
        m_copy(j).start()
        return carry

    lax.fori_loop(1, PEERS, send_meta, 0)
    loads[0].wait()

    def regroup(b, carry):
        src = pl.ds(pl.multiple_of(b * 64, 64), 64)
        dst = pl.ds(pl.multiple_of((b * 64 + mp * W) % D, 64), 64)
        w_v[:, dst, :] = jnp.swapaxes(w_raw[src], 0, 1)
        return carry

    def head(i, carry):
        @pl.when(i < GROUPS)
        def _():
            gather(i)

        @pl.when(i == 0)
        def _():
            loads[1].wait()
            lax.fori_loop(0, D // 64, regroup, 0)

        @pl.when(i >= 1)
        def _():
            norm_and_query(i - 1)

            @pl.when(i == 1)
            def _():
                q_recv[pl.ds(0, CAP), :] = q_send[pl.ds(0, CAP), :]

            send_queries(i - 1)

        return carry

    lax.fori_loop(0, GROUPS + 1, head, 0)

    for c in loads[2:]:
        c.wait()
    place = lax.broadcasted_iota(jnp.int32, (HLEN, W), 0).astype(F32)
    for user, length in ((0, len0), (1, len1)):
        kept = jnp.where(place < length, v_v[user].astype(F32), 0.0).astype(BF16)
        for n in range(HEADS_HERE):
            v01[n, :, user * HD : (user + 1) * HD] = kept[:, n * HD : (n + 1) * HD]

    pltpu.make_async_copy(
        metar.at[pl.ds(1, PEERS - 1)], metar.at[pl.ds(1, PEERS - 1)], m_rsem.at[0]
    ).wait()
    in_chunk = lax.broadcasted_iota(jnp.int32, (CAP, HD), 0).astype(F32)

    def masks(j, carry):
        mask_in[chunk_of(j), :] = jnp.where(in_chunk >= metar[j][:, 0:1], 1.0, 0.0)
        theirs = metar[mirrored(j)]
        l0, l1 = theirs[:, 64:65], theirs[:, 96:97]
        length = jnp.where(in_chunk >= meta[j][:, 0:1], l1, l0)
        inv_len[chunk_of(j), :] = 1.0 / (length + 1.0)
        return carry

    lax.fori_loop(0, PEERS, masks, 0)

    def wait_group(buf, sem, g):
        @pl.when(g == 0)
        def _():
            rows = pl.ds(ABL, (GROUP-1)*ABL)
            pltpu.make_async_copy(buf.at[rows], buf.at[rows], sem.at[0]).wait()

        @pl.when(g > 0)
        def _():
            rows = pl.ds(pl.multiple_of(g * GR, GR), GROUP * ABL)
            pltpu.make_async_copy(buf.at[rows], buf.at[rows], sem.at[g]).wait()

    def body(i, carry):
        @pl.when(i < GROUPS)
        def _():
            project_rest(i)
            wait_group(q_recv, q_rsem, i)
            attend(i)

            @pl.when(i == 0)
            def _():
                back[pl.ds(0, CAP), :] = a_send[pl.ds(0, CAP), :]

            send_back(i)

        @pl.when(jnp.logical_and(i >= LAG, i < GROUPS + LAG))
        def _():
            wait_group(back, a_rsem, i - LAG)
            finish_sums(i - LAG)

        @pl.when(jnp.logical_and(i >= LAG + 1, i < GROUPS + LAG + 1))
        def _():
            normalize(i - LAG - 1)

        @pl.when(i >= LAG + 2)
        def _():
            output(i - LAG - 2)

        return carry

    lax.fori_loop(0, GROUPS + LAG + 2, body, 0)
    out_ref[...] = acc[...].astype(BF16)

    def drain(g, carry):
        x_copy(g).wait_send()
        s_copy(g).wait_send()
        y_copy(g).wait_send()
        wait_group(q_send, q_ssem, g)
        wait_group(a_send, a_ssem, g)
        return carry

    lax.fori_loop(0, GROUPS, drain, 0)
    pltpu.make_async_copy(
        meta.at[pl.ds(1, PEERS - 1)], meta.at[pl.ds(1, PEERS - 1)], m_ssem.at[0]
    ).wait()


def body(
    candidates, cand_dest, cand_slot, hist_len, k_cache, v_cache, in_gain, w_uvqk, attn_gain, w_out
):
    vmem = pl.BlockSpec(memory_space=pltpu.VMEM)
    hbm = pl.BlockSpec(memory_space=pl.ANY)
    dma = pltpu.SemaphoreType.DMA
    return pl.pallas_call(
        kernel,
        out_shape=jax.ShapeDtypeStruct((ROWS, W), BF16),
        in_specs=[hbm, vmem, vmem, vmem, hbm, hbm, vmem, hbm, vmem, hbm],
        out_specs=vmem,
        scratch_shapes=[
            pltpu.VMEM((ROWS, W), BF16),
            pltpu.VMEM((D, 4, W), BF16),
            pltpu.VMEM((4, D, W), BF16),
            pltpu.VMEM((D, W), BF16),
            pltpu.VMEM((2, HLEN, W), BF16),
            pltpu.VMEM((2, HLEN, W), BF16),
            pltpu.VMEM((HEADS_HERE, HLEN, 2 * HD), BF16),
            pltpu.VMEM((8, ROWS), F32),
            pltpu.VMEM((ROWS, HD), F32),
            pltpu.VMEM((PEERS, 1, HD), F32),
            pltpu.VMEM((PEERS, 1, HD), F32),
            pltpu.VMEM((SLOTS, HD), F32),
            pltpu.VMEM((SLOTS, HD), F32),
            pltpu.VMEM((1, D), F32),
            pltpu.VMEM((SLOTS, W), BF16),
            pltpu.VMEM((SLOTS, W), BF16),
            pltpu.VMEM((SLOTS, D), BF16),
            pltpu.VMEM((SLOTS, W), BF16),
            pltpu.VMEM((SLOTS, W), BF16),
            pltpu.VMEM((SLOTS, W), BF16),
            pltpu.VMEM((SLOTS, W), BF16),
            pltpu.VMEM((SLOTS, W), BF16),
            pltpu.VMEM((SLOTS, W), F32),
            pltpu.VMEM((SLOTS, HD), F32),
            pltpu.VMEM((SLOTS, HD), F32),
            pltpu.VMEM((SLOTS, W), BF16),
            pltpu.VMEM((SLOTS, W), BF16),
            pltpu.VMEM((ROWS, W), F32),
            dma((6,)),
            dma((GROUPS,)), dma((GROUPS,)),
            dma((GROUPS,)), dma((GROUPS,)),
            dma((GROUPS,)), dma((GROUPS,)),
            dma((1,)), dma((1,)),
            dma((GROUPS,)), dma((GROUPS,)),
            dma((GROUPS,)), dma((GROUPS,)),
        ],
        compiler_params=pltpu.CompilerParams(
            collective_id=0, has_side_effects=True, vmem_limit_bytes=VMEM_LIMIT
        ),
        cost_estimate=pl.CostEstimate(
            flops=20 * 10**9, bytes_accessed=10 * 10**6, transcendentals=9 * 10**6
        ),
        name="routed_ranking",
    )(
        candidates,
        cand_dest.reshape(1, ROWS),
        cand_slot.reshape(1, ROWS),
        hist_len,
        k_cache,
        v_cache,
        in_gain.reshape(1, D),
        w_uvqk,
        attn_gain.reshape(1, W),
        w_out,
    )


def solution(mesh):
    return jax.shard_map(
        body,
        mesh=mesh,
        in_specs=(
            P("users", "mp"),
            P("users", None),
            P("users"),
            P("users", None),
            P("users", None, "mp"),
            P("users", None, "mp"),
            P(),
            P(None, None, "mp"),
            P("mp"),
            P(None, "mp"),
        ),
        out_specs=P("users", "mp"),
        check_vma=False,
    )
```

```python
import functools
import math

import jax
import jax.numpy as jnp
from jax import lax
from jax.experimental import pallas as pl
from jax.experimental.pallas import tpu as pltpu
from jax.sharding import PartitionSpec as P

MESH = pl.DeviceIdType.MESH
D = 1024
W = 512
HD = 128
HEADS_HERE = W // HD
HLEN = 512
ROWS = 1024
PEERS = 64
SIDE = 4
CAP = 32
SLOTS = PEERS * CAP
GROUP = 8
GROUPS = PEERS // GROUP
GR = GROUP * CAP
STEP = 37
STEP_INV = 45
LAG = 5
HOLD = 2
ORDER = 'EFG'
EPS = 1e-05
VMEM_LIMIT = 54 * 2**20
ABL = CAP
SCALE = 1.0 / math.sqrt(HD)
F32 = jnp.float32
BF16 = jnp.bfloat16


def silu(x):
    t = 0.5 * x
    return t + t * jnp.tanh(t)


def digits(k):
    return k % SIDE, (k // SIDE) % SIDE, k // (SIDE * SIDE)


def ahead(me, j):
    x, y, z = digits(me)
    a, b, c = digits((j * STEP) % PEERS)
    return ((z + c) % SIDE) * SIDE * SIDE + ((y + b) % SIDE) * SIDE + (x + a) % SIDE


def behind(me, j):
    x, y, z = digits(me)
    a, b, c = digits((j * STEP) % PEERS)
    return (
        ((z + SIDE - c) % SIDE) * SIDE * SIDE
        + ((y + SIDE - b) % SIDE) * SIDE
        + (x + SIDE - a) % SIDE
    )


def mirrored(j):
    a, b, c = digits((j * STEP) % PEERS)
    k = ((SIDE - c) % SIDE) * SIDE * SIDE + ((SIDE - b) % SIDE) * SIDE + (SIDE - a) % SIDE
    return (k * STEP_INV) % PEERS


def kernel(
    x_hbm, dest_ref, slot_ref, hist_ref, k_hbm, v_hbm, in_gain_ref, w_hbm, attn_gain_ref, wout_hbm,
    out_ref,
    x_v, w_raw, w_v, wout_v, k_v, v_v, v01, fs_row, fs_col, meta, metar, theirs, mask_in, inv_len, gain_v,
    xs_own, xs_peer, h_v, q_send, q_recv, a_send, back, u_v, self_v, st_send, st_recv,
    y_own, y_peer, acc,
    load_sem, x_ssem, x_rsem, q_ssem, q_rsem, a_ssem, a_rsem, m_ssem, m_rsem, s_ssem, s_rsem,
    y_ssem, y_rsem,
):
    me = lax.axis_index("users")
    mp = lax.axis_index("mp")
    other = 1 - mp
    own_at = pl.multiple_of(mp * W, W)
    peer_at = pl.multiple_of(other * W, W)

    barrier = pltpu.get_barrier_semaphore()

    def greet(j, carry):
        pl.semaphore_signal(barrier, inc=1, device_id=(ahead(me, j), mp), device_id_type=MESH)
        return carry

    pl.semaphore_signal(barrier, inc=1, device_id=(me, other), device_id_type=MESH)
    lax.fori_loop(1, PEERS, greet, 0)

    loads = [
        pltpu.make_async_copy(x_hbm, x_v, load_sem.at[0]),
        pltpu.make_async_copy(w_hbm, w_raw, load_sem.at[1]),
        pltpu.make_async_copy(wout_hbm.at[pl.ds(own_at, W)], wout_v.at[pl.ds(0, W)], load_sem.at[2]),
        pltpu.make_async_copy(k_hbm, k_v, load_sem.at[3]),
        pltpu.make_async_copy(v_hbm, v_v, load_sem.at[4]),
    ]
    loads.append(
        pltpu.make_async_copy(wout_hbm.at[pl.ds(peer_at, W)], wout_v.at[pl.ds(W, W)], load_sem.at[5])
    )
    for c in loads:
        c.start()

    dest = dest_ref[...]
    slot = slot_ref[...]
    mx, my, mz = digits(me)
    kx = ((dest & 3) + (SIDE - mx)) & 3
    ky = (((dest >> 2) & 3) + (SIDE - my)) & 3
    kz = ((dest >> 4) + (SIDE - mz)) & 3
    number = ((kx + 4 * ky + 16 * kz) * STEP_INV) & (PEERS - 1)
    key = 2 * number + slot
    hot = (lax.broadcasted_iota(jnp.int32, (2 * PEERS, ROWS), 0) == key).astype(F32)
    before = jnp.zeros((2 * PEERS, 256), F32)
    pos_parts = []
    tri = (
        lax.broadcasted_iota(jnp.int32, (256, 256), 0)
        < lax.broadcasted_iota(jnp.int32, (256, 256), 1)
    ).astype(F32).astype(BF16)
    count = jnp.zeros((2 * PEERS, 1), F32)
    for b in range(ROWS // 256):
        part = hot[:, b * 256 : (b + 1) * 256]
        before = jnp.dot(part.astype(BF16), tri, preferred_element_type=F32) + count
        pos_parts.append(jnp.sum(before * part, axis=0, keepdims=True))
        count = count + jnp.sum(part, axis=1, keepdims=True)
    pos = jnp.concatenate(pos_parts, axis=1)
    fs = (number * CAP).astype(F32) + jnp.where(slot == 0, pos, (CAP - 1) - pos)
    fs_row[...] = jnp.broadcast_to(fs, (8, ROWS))

    def rows_of(g):
        return pl.ds(pl.multiple_of(g * GR, GR), GR)

    def chunk_of(j):
        return pl.ds(pl.multiple_of(j * CAP, CAP), CAP)

    def abl_of(j):
        return pl.ds(pl.multiple_of(j * CAP, CAP), ABL)

    def x_copy(g):
        return pltpu.make_async_remote_copy(
            src_ref=xs_own.at[rows_of(g)], dst_ref=xs_peer.at[rows_of(g)],
            send_sem=x_ssem.at[g], recv_sem=x_rsem.at[g],
            device_id=(me, other), device_id_type=MESH,
        )

    def q_copy(g, j):
        return pltpu.make_async_remote_copy(
            src_ref=q_send.at[abl_of(j)], dst_ref=q_recv.at[abl_of(j)],
            send_sem=q_ssem.at[g], recv_sem=q_rsem.at[g],
            device_id=(ahead(me, j), mp), device_id_type=MESH,
        )

    def a_copy(g, j):
        return pltpu.make_async_remote_copy(
            src_ref=a_send.at[abl_of(j)], dst_ref=back.at[abl_of(j)],
            send_sem=a_ssem.at[g], recv_sem=a_rsem.at[g],
            device_id=(behind(me, j), mp), device_id_type=MESH,
        )

    def s_copy(g):
        return pltpu.make_async_remote_copy(
            src_ref=st_send.at[rows_of(g)], dst_ref=st_recv.at[rows_of(g)],
            send_sem=s_ssem.at[g], recv_sem=s_rsem.at[g],
            device_id=(me, other), device_id_type=MESH,
        )

    def y_copy(g):
        return pltpu.make_async_remote_copy(
            src_ref=y_own.at[rows_of(g)], dst_ref=y_peer.at[rows_of(g)],
            send_sem=y_ssem.at[g], recv_sem=y_rsem.at[g],
            device_id=(me, other), device_id_type=MESH,
        )

    def m_copy(j):
        return pltpu.make_async_remote_copy(
            src_ref=meta.at[j], dst_ref=metar.at[j],
            send_sem=m_ssem.at[0], recv_sem=m_rsem.at[0],
            device_id=(ahead(me, j), mp), device_id_type=MESH,
        )

    def gather(g):
        slots = lax.broadcasted_iota(jnp.int32, (GR, ROWS), 0).astype(F32) + (g * GR).astype(F32)
        pick = jnp.where(slots == fs_row[0:1, :], 1.0, 0.0).astype(BF16)
        xs_own[rows_of(g), :] = jnp.dot(pick, x_v[...], preferred_element_type=F32).astype(BF16)

    def norm_and_query(g):
        x_copy(g).wait_recv()
        xo = xs_own[rows_of(g), :].astype(F32)
        xp = xs_peer[rows_of(g), :].astype(F32)
        xf = jnp.concatenate([xo, xp], axis=1)
        mean = jnp.sum(xf, axis=1, keepdims=True) * (1.0 / D)
        c = xf - mean
        var = jnp.sum(c * c, axis=1, keepdims=True) * (1.0 / D)
        h = (c * lax.rsqrt(var + EPS) * gain_v[...]).astype(BF16)
        h_v[rows_of(g), :] = h
        q_send[rows_of(g), :] = silu(jnp.dot(h, w_v[2], preferred_element_type=F32)).astype(BF16)

    def send_queries(g):
        lo = jnp.where(g == 0, 1, g * GROUP)

        def one(j, carry):
            q_copy(g, j).start()
            return carry

        lax.fori_loop(lo, (g + 1) * GROUP, one, 0)

    def project_rest(g):
        h = h_v[rows_of(g), :]
        u_v[rows_of(g), :] = silu(jnp.dot(h, w_v[0], preferred_element_type=F32)).astype(BF16)
        v = silu(jnp.dot(h, w_v[1], preferred_element_type=F32)).astype(BF16).astype(F32)
        k = silu(jnp.dot(h, w_v[3], preferred_element_type=F32)).astype(BF16).astype(F32)
        q = q_send[rows_of(g), :].astype(F32)
        qk = q * k
        for n in range(HEADS_HERE):
            cols = slice(n * HD, (n + 1) * HD)
            s = jnp.sum(qk[:, cols], axis=1, keepdims=True) * SCALE
            sw = silu(s).astype(BF16).astype(F32)
            self_v[rows_of(g), cols] = sw * v[:, cols] * inv_len[rows_of(g), :]

    def attend(g):
        m1 = mask_in[rows_of(g), :]
        m0 = 1.0 - m1
        rs = m0 * (1.0 / (len0 + 1.0)) + m1 * (1.0 / (len1 + 1.0))
        for n in range(HEADS_HERE):
            cols = slice(n * HD, (n + 1) * HD)
            qf = q_recv[rows_of(g), cols].astype(F32)
            q01 = jnp.concatenate([(qf * m0).astype(BF16), (qf * m1).astype(BF16)], axis=1)
            k01 = jnp.concatenate([k_v[0, :, cols], k_v[1, :, cols]], axis=1)
            s = lax.dot_general(q01, k01, (((1,), (1,)), ((), ())), preferred_element_type=F32)
            t = s * (0.5 * SCALE)
            wts = (t + t * jnp.tanh(t)).astype(BF16)
            o = jnp.dot(wts, v01[n], preferred_element_type=F32)
            a = (o[:, :HD] * m0 + o[:, HD:] * m1) * rs
            a_send[rows_of(g), cols] = a.astype(BF16)

    def send_back(g):
        lo = jnp.where(g == 0, 1, g * GROUP)

        def one(j, carry):
            a_copy(g, j).start()
            return carry

        lax.fori_loop(lo, (g + 1) * GROUP, one, 0)

    def finish_sums(g):
        a = back[rows_of(g), :].astype(F32) + self_v[rows_of(g), :]
        mean = jnp.sum(a, axis=1, keepdims=True) * (1.0 / W)
        c = a - mean
        m2 = jnp.sum(c * c, axis=1, keepdims=True)
        self_v[rows_of(g), :] = a
        lanes = lax.broadcasted_iota(jnp.int32, (GR, HD), 1)
        st_send[rows_of(g), :] = jnp.where(lanes < 64, mean, m2)
        s_copy(g).start()

    def normalize(g):
        s_copy(g).wait_recv()
        so = st_send[rows_of(g), :]
        sp = st_recv[rows_of(g), :]
        mo, mp_ = so[:, 0:1], sp[:, 0:1]
        mean = 0.5 * (mo + mp_)
        gap = mo - mp_
        var = (so[:, 64:65] + sp[:, 64:65] + (0.5 * W) * gap * gap) * (1.0 / D)
        y = (
            (self_v[rows_of(g), :] - mean)
            * lax.rsqrt(var + EPS)
            * attn_gain_ref[...]
            * u_v[rows_of(g), :].astype(F32)
        )
        y_own[rows_of(g), :] = y.astype(BF16)
        y_copy(g).start()

    def output(g):
        y_copy(g).wait_recv()
        y = jnp.concatenate([y_own[rows_of(g), :], y_peer[rows_of(g), :]], axis=1)
        p = jnp.dot(y, wout_v[...], preferred_element_type=F32)
        fin = (xs_own[rows_of(g), :].astype(F32) + p).astype(BF16)
        base = (g * GR).astype(F32)
        lanes = lax.broadcasted_iota(jnp.int32, (ROWS, HD), 1).astype(F32) + base
        f = fs_col[...]
        pick = jnp.concatenate(
            [jnp.where(f == lanes + float(n * HD), 1.0, 0.0).astype(BF16) for n in range(GR // HD)],
            axis=1,
        )
        acc[...] += jnp.dot(pick, fin, preferred_element_type=F32)

    loads[0].wait()
    gather(jnp.int32(0))
    pl.semaphore_wait(barrier, PEERS)
    x_copy(0).start()

    fs_col[...] = jnp.broadcast_to(fs, (HD, ROWS)).T
    same = lax.broadcasted_iota(jnp.int32, (PEERS, ROWS), 0) == number
    first = jnp.sum(jnp.where(same & (slot == 0), 1.0, 0.0), axis=1, keepdims=True)
    hist = hist_ref[...].astype(F32)
    len0, len1 = hist[:, 0:1], hist[:, 1:2]
    lane = lax.broadcasted_iota(jnp.int32, (PEERS, HD), 1)
    meta_rows = jnp.where(lane < 64, first, jnp.where(lane < 96, len0, len1))
    meta[...] = meta_rows.reshape(PEERS, 1, HD)
    metar[0] = meta[0]
    gain_v[...] = jnp.concatenate(
        [in_gain_ref[:, pl.ds(own_at, W)], in_gain_ref[:, pl.ds(peer_at, W)]], axis=1
    )
    acc[...] = jnp.zeros_like(acc)

    def send_meta(j, carry):
        m_copy(j).start()
        return carry

    lax.fori_loop(1, PEERS, send_meta, 0)

    def regroup(b, carry):
        src = pl.ds(pl.multiple_of(b * 64, 64), 64)
        dst = pl.ds(pl.multiple_of((b * 64 + mp * W) % D, 64), 64)
        w_v[:, dst, :] = jnp.swapaxes(w_raw[src], 0, 1)
        return carry

    loads[1].wait()
    lax.fori_loop(0, D // 64, regroup, 0)

    def head(i, carry):
        @pl.when(i < GROUPS)
        def _():
            gather(i)
            x_copy(i).start()

        norm_and_query(i - 1)

        @pl.when(i == 1)
        def _():
            q_recv[pl.ds(0, CAP), :] = q_send[pl.ds(0, CAP), :]

        send_queries(i - 1)
        return carry

    lax.fori_loop(1, GROUPS + 1, head, 0)

    for c in loads[2:]:
        c.wait()
    place = lax.broadcasted_iota(jnp.int32, (HLEN, W), 0).astype(F32)
    for user, length in ((0, len0), (1, len1)):
        kept = jnp.where(place < length, v_v[user].astype(F32), 0.0).astype(BF16)
        for n in range(HEADS_HERE):
            v01[n, :, user * HD : (user + 1) * HD] = kept[:, n * HD : (n + 1) * HD]

    pltpu.make_async_copy(
        metar.at[pl.ds(1, PEERS - 1)], metar.at[pl.ds(1, PEERS - 1)], m_rsem.at[0]
    ).wait()
    for j in range(PEERS):
        theirs[j] = metar[mirrored(j)]
    in_chunk = lax.broadcasted_iota(jnp.int32, (PEERS, CAP, HD), 1).astype(F32)
    mask_in[...] = jnp.where(in_chunk >= metar[...][:, :, 0:1], 1.0, 0.0).reshape(SLOTS, HD)
    inv = 1.0 / (theirs[...] + 1.0)
    inv_len[...] = jnp.where(
        in_chunk >= meta[...][:, :, 0:1], inv[:, :, 96:97], inv[:, :, 64:65]
    ).reshape(SLOTS, HD)

    def wait_group(buf, sem, g):
        @pl.when(g == 0)
        def _():
            rows = pl.ds(ABL, (GROUP-1)*ABL)
            pltpu.make_async_copy(buf.at[rows], buf.at[rows], sem.at[0]).wait()

        @pl.when(g > 0)
        def _():
            rows = pl.ds(pl.multiple_of(g * GR, GR), GROUP * ABL)
            pltpu.make_async_copy(buf.at[rows], buf.at[rows], sem.at[g]).wait()

    def body(i, carry):
        @pl.when(i < GROUPS)
        def _():
            project_rest(i)
            wait_group(q_recv, q_rsem, i)
            attend(i)

            @pl.when(i == 0)
            def _():
                back[pl.ds(0, CAP), :] = a_send[pl.ds(0, CAP), :]

        @pl.when(jnp.logical_and(i >= HOLD, i < GROUPS + HOLD))
        def _():
            send_back(i - HOLD)

        def out_step():
            @pl.when(jnp.logical_and(i >= LAG + 2, i < GROUPS + LAG + 2))
            def _():
                output(i - LAG - 2)

        def norm_step():
            @pl.when(jnp.logical_and(i >= LAG + 1, i < GROUPS + LAG + 1))
            def _():
                normalize(i - LAG - 1)

        def sum_step():
            @pl.when(jnp.logical_and(i >= LAG, i < GROUPS + LAG))
            def _():
                wait_group(back, a_rsem, i - LAG)
                finish_sums(i - LAG)

        steps = dict(E=sum_step, F=norm_step, G=out_step)
        for name in ORDER:
            steps[name]()

        return carry

    lax.fori_loop(0, GROUPS + LAG + 2, body, 0)
    out_ref[...] = acc[...].astype(BF16)

    def drain(g, carry):
        x_copy(g).wait_send()
        s_copy(g).wait_send()
        y_copy(g).wait_send()
        wait_group(q_send, q_ssem, g)
        wait_group(a_send, a_ssem, g)
        return carry

    lax.fori_loop(0, GROUPS, drain, 0)
    pltpu.make_async_copy(
        meta.at[pl.ds(1, PEERS - 1)], meta.at[pl.ds(1, PEERS - 1)], m_ssem.at[0]
    ).wait()


def body(
    candidates, cand_dest, cand_slot, hist_len, k_cache, v_cache, in_gain, w_uvqk, attn_gain, w_out
):
    vmem = pl.BlockSpec(memory_space=pltpu.VMEM)
    hbm = pl.BlockSpec(memory_space=pl.ANY)
    dma = pltpu.SemaphoreType.DMA
    return pl.pallas_call(
        kernel,
        out_shape=jax.ShapeDtypeStruct((ROWS, W), BF16),
        in_specs=[hbm, vmem, vmem, vmem, hbm, hbm, vmem, hbm, vmem, hbm],
        out_specs=vmem,
        scratch_shapes=[
            pltpu.VMEM((ROWS, W), BF16),
            pltpu.VMEM((D, 4, W), BF16),
            pltpu.VMEM((4, D, W), BF16),
            pltpu.VMEM((D, W), BF16),
            pltpu.VMEM((2, HLEN, W), BF16),
            pltpu.VMEM((2, HLEN, W), BF16),
            pltpu.VMEM((HEADS_HERE, HLEN, 2 * HD), BF16),
            pltpu.VMEM((8, ROWS), F32),
            pltpu.VMEM((ROWS, HD), F32),
            pltpu.VMEM((PEERS, 1, HD), F32),
            pltpu.VMEM((PEERS, 1, HD), F32),
            pltpu.VMEM((PEERS, 1, HD), F32),
            pltpu.VMEM((SLOTS, HD), F32),
            pltpu.VMEM((SLOTS, HD), F32),
            pltpu.VMEM((1, D), F32),
            pltpu.VMEM((SLOTS, W), BF16),
            pltpu.VMEM((SLOTS, W), BF16),
            pltpu.VMEM((SLOTS, D), BF16),
            pltpu.VMEM((SLOTS, W), BF16),
            pltpu.VMEM((SLOTS, W), BF16),
            pltpu.VMEM((SLOTS, W), BF16),
            pltpu.VMEM((SLOTS, W), BF16),
            pltpu.VMEM((SLOTS, W), BF16),
            pltpu.VMEM((SLOTS, W), F32),
            pltpu.VMEM((SLOTS, HD), F32),
            pltpu.VMEM((SLOTS, HD), F32),
            pltpu.VMEM((SLOTS, W), BF16),
            pltpu.VMEM((SLOTS, W), BF16),
            pltpu.VMEM((ROWS, W), F32),
            dma((6,)),
            dma((GROUPS,)), dma((GROUPS,)),
            dma((GROUPS,)), dma((GROUPS,)),
            dma((GROUPS,)), dma((GROUPS,)),
            dma((1,)), dma((1,)),
            dma((GROUPS,)), dma((GROUPS,)),
            dma((GROUPS,)), dma((GROUPS,)),
        ],
        compiler_params=pltpu.CompilerParams(
            collective_id=0, has_side_effects=True, vmem_limit_bytes=VMEM_LIMIT
        ),
        cost_estimate=pl.CostEstimate(
            flops=20 * 10**9, bytes_accessed=10 * 10**6, transcendentals=9 * 10**6
        ),
        name="routed_ranking",
    )(
        candidates,
        cand_dest.reshape(1, ROWS),
        cand_slot.reshape(1, ROWS),
        hist_len,
        k_cache,
        v_cache,
        in_gain.reshape(1, D),
        w_uvqk,
        attn_gain.reshape(1, W),
        w_out,
    )


def solution(mesh):
    return jax.shard_map(
        body,
        mesh=mesh,
        in_specs=(
            P("users", "mp"),
            P("users", None),
            P("users"),
            P("users", None),
            P("users", None, "mp"),
            P("users", None, "mp"),
            P(),
            P(None, None, "mp"),
            P("mp"),
            P(None, "mp"),
        ),
        out_specs=P("users", "mp"),
        check_vma=False,
    )
```

```python
import functools
import math

import jax
import jax.numpy as jnp
from jax import lax
from jax.experimental import pallas as pl
from jax.experimental.pallas import tpu as pltpu
from jax.sharding import PartitionSpec as P

MESH = pl.DeviceIdType.MESH
D = 1024
W = 512
HD = 128
HEADS_HERE = W // HD
HLEN = 512
ROWS = 1024
PEERS = 64
SIDE = 4
CAP = 32
SLOTS = PEERS * CAP
GROUP = 8
GROUPS = PEERS // GROUP
GR = GROUP * CAP
STEP = 37
STEP_INV = 45
LAG = 5
HOLD = 2
ORDER = 'EFG'
EPS = 1e-05
VMEM_LIMIT = 54 * 2**20
ABL = CAP
SCALE = 1.0 / math.sqrt(HD)
F32 = jnp.float32
BF16 = jnp.bfloat16


def silu(x):
    t = 0.5 * x
    return t + t * jnp.tanh(t)


def digits(k):
    return k % SIDE, (k // SIDE) % SIDE, k // (SIDE * SIDE)


def ahead(me, j):
    x, y, z = digits(me)
    a, b, c = digits((j * STEP) % PEERS)
    return ((z + c) % SIDE) * SIDE * SIDE + ((y + b) % SIDE) * SIDE + (x + a) % SIDE


def behind(me, j):
    x, y, z = digits(me)
    a, b, c = digits((j * STEP) % PEERS)
    return (
        ((z + SIDE - c) % SIDE) * SIDE * SIDE
        + ((y + SIDE - b) % SIDE) * SIDE
        + (x + SIDE - a) % SIDE
    )


def mirrored(j):
    a, b, c = digits((j * STEP) % PEERS)
    k = ((SIDE - c) % SIDE) * SIDE * SIDE + ((SIDE - b) % SIDE) * SIDE + (SIDE - a) % SIDE
    return (k * STEP_INV) % PEERS


def kernel(
    x_hbm, dest_ref, slot_ref, hist_ref, k_hbm, v_hbm, in_gain_ref, w_hbm, attn_gain_ref, wout_hbm,
    out_ref,
    x_v, w_raw, w_v, wout_v, k_v, v_v, v01, fs_row, fs_col, meta, metar, theirs, mask_in, inv_len, gain_v,
    xs_own, xs_peer, h_v, q_send, q_recv, a_send, back, u_v, self_v, st_send, st_recv,
    y_own, y_peer, acc,
    load_sem, x_ssem, x_rsem, q_ssem, q_rsem, a_ssem, a_rsem, m_ssem, m_rsem, s_ssem, s_rsem,
    y_ssem, y_rsem,
):
    me = lax.axis_index("users")
    mp = lax.axis_index("mp")
    other = 1 - mp
    own_at = pl.multiple_of(mp * W, W)
    peer_at = pl.multiple_of(other * W, W)

    barrier = pltpu.get_barrier_semaphore()

    def greet(j, carry):
        pl.semaphore_signal(barrier, inc=1, device_id=(ahead(me, j), mp), device_id_type=MESH)
        return carry

    pl.semaphore_signal(barrier, inc=1, device_id=(me, other), device_id_type=MESH)
    lax.fori_loop(1, PEERS, greet, 0)

    loads = [
        pltpu.make_async_copy(x_hbm, x_v, load_sem.at[0]),
        pltpu.make_async_copy(w_hbm, w_raw, load_sem.at[1]),
        pltpu.make_async_copy(wout_hbm.at[pl.ds(own_at, W)], wout_v.at[pl.ds(0, W)], load_sem.at[2]),
        pltpu.make_async_copy(k_hbm, k_v, load_sem.at[3]),
        pltpu.make_async_copy(v_hbm, v_v, load_sem.at[4]),
    ]
    loads.append(
        pltpu.make_async_copy(wout_hbm.at[pl.ds(peer_at, W)], wout_v.at[pl.ds(W, W)], load_sem.at[5])
    )
    for c in loads:
        c.start()

    dest = dest_ref[...]
    slot = slot_ref[...]
    mx, my, mz = digits(me)
    kx = ((dest & 3) + (SIDE - mx)) & 3
    ky = (((dest >> 2) & 3) + (SIDE - my)) & 3
    kz = ((dest >> 4) + (SIDE - mz)) & 3
    number = ((kx + 4 * ky + 16 * kz) * STEP_INV) & (PEERS - 1)
    key = 2 * number + slot
    hot = (lax.broadcasted_iota(jnp.int32, (2 * PEERS, ROWS), 0) == key).astype(F32)
    before = jnp.zeros((2 * PEERS, 256), F32)
    pos_parts = []
    tri = (
        lax.broadcasted_iota(jnp.int32, (256, 256), 0)
        < lax.broadcasted_iota(jnp.int32, (256, 256), 1)
    ).astype(F32).astype(BF16)
    count = jnp.zeros((2 * PEERS, 1), F32)
    for b in range(ROWS // 256):
        part = hot[:, b * 256 : (b + 1) * 256]
        before = jnp.dot(part.astype(BF16), tri, preferred_element_type=F32) + count
        pos_parts.append(jnp.sum(before * part, axis=0, keepdims=True))
        count = count + jnp.sum(part, axis=1, keepdims=True)
    pos = jnp.concatenate(pos_parts, axis=1)
    fs = (number * CAP).astype(F32) + jnp.where(slot == 0, pos, (CAP - 1) - pos)
    fs_row[...] = jnp.broadcast_to(fs, (8, ROWS))

    def rows_of(g):
        return pl.ds(pl.multiple_of(g * GR, GR), GR)

    def chunk_of(j):
        return pl.ds(pl.multiple_of(j * CAP, CAP), CAP)

    def abl_of(j):
        return pl.ds(pl.multiple_of(j * CAP, CAP), ABL)

    def x_copy(g):
        return pltpu.make_async_remote_copy(
            src_ref=xs_own.at[rows_of(g)], dst_ref=xs_peer.at[rows_of(g)],
            send_sem=x_ssem.at[g], recv_sem=x_rsem.at[g],
            device_id=(me, other), device_id_type=MESH,
        )

    def q_copy(g, j):
        return pltpu.make_async_remote_copy(
            src_ref=q_send.at[abl_of(j)], dst_ref=q_recv.at[abl_of(j)],
            send_sem=q_ssem.at[g], recv_sem=q_rsem.at[g],
            device_id=(ahead(me, j), mp), device_id_type=MESH,
        )

    def a_copy(g, j):
        return pltpu.make_async_remote_copy(
            src_ref=a_send.at[abl_of(j)], dst_ref=back.at[abl_of(j)],
            send_sem=a_ssem.at[g], recv_sem=a_rsem.at[g],
            device_id=(behind(me, j), mp), device_id_type=MESH,
        )

    def s_copy(g):
        return pltpu.make_async_remote_copy(
            src_ref=st_send.at[rows_of(g)], dst_ref=st_recv.at[rows_of(g)],
            send_sem=s_ssem.at[g], recv_sem=s_rsem.at[g],
            device_id=(me, other), device_id_type=MESH,
        )

    def y_copy(g):
        return pltpu.make_async_remote_copy(
            src_ref=y_own.at[rows_of(g)], dst_ref=y_peer.at[rows_of(g)],
            send_sem=y_ssem.at[g], recv_sem=y_rsem.at[g],
            device_id=(me, other), device_id_type=MESH,
        )

    def m_copy(j):
        return pltpu.make_async_remote_copy(
            src_ref=meta.at[j], dst_ref=metar.at[j],
            send_sem=m_ssem.at[0], recv_sem=m_rsem.at[0],
            device_id=(ahead(me, j), mp), device_id_type=MESH,
        )

    def gather(g):
        slots = lax.broadcasted_iota(jnp.int32, (GR, ROWS), 0).astype(F32) + (g * GR).astype(F32)
        pick = jnp.where(slots == fs_row[0:1, :], 1.0, 0.0).astype(BF16)
        xs_own[rows_of(g), :] = jnp.dot(pick, x_v[...], preferred_element_type=F32).astype(BF16)

    def norm_and_query(g):
        x_copy(g).wait_recv()
        xo = xs_own[rows_of(g), :].astype(F32)
        xp = xs_peer[rows_of(g), :].astype(F32)
        xf = jnp.concatenate([xo, xp], axis=1)
        mean = jnp.sum(xf, axis=1, keepdims=True) * (1.0 / D)
        c = xf - mean
        var = jnp.sum(c * c, axis=1, keepdims=True) * (1.0 / D)
        h = (c * lax.rsqrt(var + EPS) * gain_v[...]).astype(BF16)
        h_v[rows_of(g), :] = h
        q_send[rows_of(g), :] = silu(jnp.dot(h, w_v[2], preferred_element_type=F32)).astype(BF16)

    def send_queries(g):
        lo = jnp.where(g == 0, 1, g * GROUP)

        def one(j, carry):
            q_copy(g, j).start()
            return carry

        lax.fori_loop(lo, (g + 1) * GROUP, one, 0)

    def project_rest(g):
        h = h_v[rows_of(g), :]
        u_v[rows_of(g), :] = silu(jnp.dot(h, w_v[0], preferred_element_type=F32)).astype(BF16)
        v = silu(jnp.dot(h, w_v[1], preferred_element_type=F32)).astype(BF16).astype(F32)
        k = silu(jnp.dot(h, w_v[3], preferred_element_type=F32)).astype(BF16).astype(F32)
        q = q_send[rows_of(g), :].astype(F32)
        qk = q * k
        for n in range(HEADS_HERE):
            cols = slice(n * HD, (n + 1) * HD)
            s = jnp.sum(qk[:, cols], axis=1, keepdims=True) * SCALE
            sw = silu(s).astype(BF16).astype(F32)
            self_v[rows_of(g), cols] = sw * v[:, cols] * inv_len[rows_of(g), :]

    def attend(g):
        m1 = mask_in[rows_of(g), :]
        m0 = 1.0 - m1
        rs = m0 * (1.0 / (len0 + 1.0)) + m1 * (1.0 / (len1 + 1.0))
        for n in range(HEADS_HERE):
            cols = slice(n * HD, (n + 1) * HD)
            qf = q_recv[rows_of(g), cols].astype(F32)
            q01 = jnp.concatenate([(qf * m0).astype(BF16), (qf * m1).astype(BF16)], axis=1)
            k01 = jnp.concatenate([k_v[0, :, cols], k_v[1, :, cols]], axis=1)
            s = lax.dot_general(q01, k01, (((1,), (1,)), ((), ())), preferred_element_type=F32)
            t = s * (0.5 * SCALE)
            wts = (t + t * jnp.tanh(t)).astype(BF16)
            o = jnp.dot(wts, v01[n], preferred_element_type=F32)
            a = (o[:, :HD] * m0 + o[:, HD:] * m1) * rs
            a_send[rows_of(g), cols] = a.astype(BF16)

    def send_back(g):
        lo = jnp.where(g == 0, 1, g * GROUP)

        def one(j, carry):
            a_copy(g, j).start()
            return carry

        lax.fori_loop(lo, (g + 1) * GROUP, one, 0)

    def finish_sums(g):
        a = back[rows_of(g), :].astype(F32) + self_v[rows_of(g), :]
        mean = jnp.sum(a, axis=1, keepdims=True) * (1.0 / W)
        c = a - mean
        m2 = jnp.sum(c * c, axis=1, keepdims=True)
        self_v[rows_of(g), :] = a
        lanes = lax.broadcasted_iota(jnp.int32, (GR, HD), 1)
        st_send[rows_of(g), :] = jnp.where(lanes < 64, mean, m2)
        s_copy(g).start()

    def normalize(g):
        s_copy(g).wait_recv()
        so = st_send[rows_of(g), :]
        sp = st_recv[rows_of(g), :]
        mo, mp_ = so[:, 0:1], sp[:, 0:1]
        mean = 0.5 * (mo + mp_)
        gap = mo - mp_
        var = (so[:, 64:65] + sp[:, 64:65] + (0.5 * W) * gap * gap) * (1.0 / D)
        y = (
            (self_v[rows_of(g), :] - mean)
            * lax.rsqrt(var + EPS)
            * attn_gain_ref[...]
            * u_v[rows_of(g), :].astype(F32)
        )
        y_own[rows_of(g), :] = y.astype(BF16)
        y_copy(g).start()

    def output(g):
        y_copy(g).wait_recv()
        y = jnp.concatenate([y_own[rows_of(g), :], y_peer[rows_of(g), :]], axis=1)
        p = jnp.dot(y, wout_v[...], preferred_element_type=F32)
        fin = (xs_own[rows_of(g), :].astype(F32) + p).astype(BF16)
        base = (g * GR).astype(F32)
        lanes = lax.broadcasted_iota(jnp.int32, (ROWS, HD), 1).astype(F32) + base
        f = fs_col[...]
        pick = jnp.concatenate(
            [jnp.where(f == lanes + float(n * HD), 1.0, 0.0).astype(BF16) for n in range(GR // HD)],
            axis=1,
        )
        acc[...] += jnp.dot(pick, fin, preferred_element_type=F32)

    loads[0].wait()
    gather(jnp.int32(0))
    pl.semaphore_wait(barrier, PEERS)
    x_copy(0).start()

    fs_col[...] = jnp.broadcast_to(fs, (HD, ROWS)).T
    same = lax.broadcasted_iota(jnp.int32, (PEERS, ROWS), 0) == number
    first = jnp.sum(jnp.where(same & (slot == 0), 1.0, 0.0), axis=1, keepdims=True)
    hist = hist_ref[...].astype(F32)
    len0, len1 = hist[:, 0:1], hist[:, 1:2]
    lane = lax.broadcasted_iota(jnp.int32, (PEERS, HD), 1)
    meta_rows = jnp.where(lane < 64, first, jnp.where(lane < 96, len0, len1))
    meta[...] = meta_rows.reshape(PEERS, 1, HD)
    metar[0] = meta[0]
    gain_v[...] = jnp.concatenate(
        [in_gain_ref[:, pl.ds(own_at, W)], in_gain_ref[:, pl.ds(peer_at, W)]], axis=1
    )
    acc[...] = jnp.zeros_like(acc)

    def send_meta(j, carry):
        m_copy(j).start()
        return carry

    lax.fori_loop(1, PEERS, send_meta, 0)

    def regroup(b, carry):
        src = pl.ds(pl.multiple_of(b * 64, 64), 64)
        dst = pl.ds(pl.multiple_of((b * 64 + mp * W) % D, 64), 64)
        w_v[:, dst, :] = jnp.swapaxes(w_raw[src], 0, 1)
        return carry

    loads[1].wait()
    lax.fori_loop(0, D // 64, regroup, 0)

    def head(i, carry):
        @pl.when(i < GROUPS)
        def _():
            gather(i)
            x_copy(i).start()

        norm_and_query(i - 1)

        @pl.when(i == 1)
        def _():
            q_recv[pl.ds(0, CAP), :] = q_send[pl.ds(0, CAP), :]

        send_queries(i - 1)
        return carry

    lax.fori_loop(1, GROUPS + 1, head, 0)

    for c in loads[2:]:
        c.wait()
    place = lax.broadcasted_iota(jnp.int32, (HLEN, W), 0).astype(F32)
    for user, length in ((0, len0), (1, len1)):
        kept = jnp.where(place < length, v_v[user].astype(F32), 0.0).astype(BF16)
        for n in range(HEADS_HERE):
            v01[n, :, user * HD : (user + 1) * HD] = kept[:, n * HD : (n + 1) * HD]

    pltpu.make_async_copy(
        metar.at[pl.ds(1, PEERS - 1)], metar.at[pl.ds(1, PEERS - 1)], m_rsem.at[0]
    ).wait()
    for j in range(PEERS):
        theirs[j] = metar[mirrored(j)]
    in_chunk = lax.broadcasted_iota(jnp.int32, (PEERS, CAP, HD), 1).astype(F32)
    mask_in[...] = jnp.where(in_chunk >= metar[...][:, :, 0:1], 1.0, 0.0).reshape(SLOTS, HD)
    inv = 1.0 / (theirs[...] + 1.0)
    inv_len[...] = jnp.where(
        in_chunk >= meta[...][:, :, 0:1], inv[:, :, 96:97], inv[:, :, 64:65]
    ).reshape(SLOTS, HD)

    def wait_group(buf, sem, g):
        @pl.when(g == 0)
        def _():
            rows = pl.ds(ABL, (GROUP-1)*ABL)
            pltpu.make_async_copy(buf.at[rows], buf.at[rows], sem.at[0]).wait()

        @pl.when(g > 0)
        def _():
            rows = pl.ds(pl.multiple_of(g * GR, GR), GROUP * ABL)
            pltpu.make_async_copy(buf.at[rows], buf.at[rows], sem.at[g]).wait()

    def body(i, carry):
        @pl.when(i < GROUPS)
        def _():
            project_rest(i)
            wait_group(q_recv, q_rsem, i)
            attend(i)

            @pl.when(i == 0)
            def _():
                back[pl.ds(0, CAP), :] = a_send[pl.ds(0, CAP), :]

        @pl.when(jnp.logical_and(i >= HOLD, i < GROUPS))
        def _():
            send_back(i - HOLD)

        @pl.when(i == GROUPS - 1)
        def _():
            for g in range(GROUPS - HOLD, GROUPS):
                send_back(jnp.int32(g))

        def out_step():
            @pl.when(jnp.logical_and(i >= LAG + 2, i < GROUPS + LAG + 2))
            def _():
                output(i - LAG - 2)

        def norm_step():
            @pl.when(jnp.logical_and(i >= LAG + 1, i < GROUPS + LAG + 1))
            def _():
                normalize(i - LAG - 1)

        def sum_step():
            @pl.when(jnp.logical_and(i >= LAG, i < GROUPS + LAG))
            def _():
                wait_group(back, a_rsem, i - LAG)
                finish_sums(i - LAG)

        steps = dict(E=sum_step, F=norm_step, G=out_step)
        for name in ORDER:
            steps[name]()

        return carry

    lax.fori_loop(0, GROUPS + LAG + 2, body, 0)
    out_ref[...] = acc[...].astype(BF16)

    def drain(g, carry):
        x_copy(g).wait_send()
        s_copy(g).wait_send()
        y_copy(g).wait_send()
        wait_group(q_send, q_ssem, g)
        wait_group(a_send, a_ssem, g)
        return carry

    lax.fori_loop(0, GROUPS, drain, 0)
    pltpu.make_async_copy(
        meta.at[pl.ds(1, PEERS - 1)], meta.at[pl.ds(1, PEERS - 1)], m_ssem.at[0]
    ).wait()


def body(
    candidates, cand_dest, cand_slot, hist_len, k_cache, v_cache, in_gain, w_uvqk, attn_gain, w_out
):
    vmem = pl.BlockSpec(memory_space=pltpu.VMEM)
    hbm = pl.BlockSpec(memory_space=pl.ANY)
    dma = pltpu.SemaphoreType.DMA
    return pl.pallas_call(
        kernel,
        out_shape=jax.ShapeDtypeStruct((ROWS, W), BF16),
        in_specs=[hbm, vmem, vmem, vmem, hbm, hbm, vmem, hbm, vmem, hbm],
        out_specs=vmem,
        scratch_shapes=[
            pltpu.VMEM((ROWS, W), BF16),
            pltpu.VMEM((D, 4, W), BF16),
            pltpu.VMEM((4, D, W), BF16),
            pltpu.VMEM((D, W), BF16),
            pltpu.VMEM((2, HLEN, W), BF16),
            pltpu.VMEM((2, HLEN, W), BF16),
            pltpu.VMEM((HEADS_HERE, HLEN, 2 * HD), BF16),
            pltpu.VMEM((8, ROWS), F32),
            pltpu.VMEM((ROWS, HD), F32),
            pltpu.VMEM((PEERS, 1, HD), F32),
            pltpu.VMEM((PEERS, 1, HD), F32),
            pltpu.VMEM((PEERS, 1, HD), F32),
            pltpu.VMEM((SLOTS, HD), F32),
            pltpu.VMEM((SLOTS, HD), F32),
            pltpu.VMEM((1, D), F32),
            pltpu.VMEM((SLOTS, W), BF16),
            pltpu.VMEM((SLOTS, W), BF16),
            pltpu.VMEM((SLOTS, D), BF16),
            pltpu.VMEM((SLOTS, W), BF16),
            pltpu.VMEM((SLOTS, W), BF16),
            pltpu.VMEM((SLOTS, W), BF16),
            pltpu.VMEM((SLOTS, W), BF16),
            pltpu.VMEM((SLOTS, W), BF16),
            pltpu.VMEM((SLOTS, W), F32),
            pltpu.VMEM((SLOTS, HD), F32),
            pltpu.VMEM((SLOTS, HD), F32),
            pltpu.VMEM((SLOTS, W), BF16),
            pltpu.VMEM((SLOTS, W), BF16),
            pltpu.VMEM((ROWS, W), F32),
            dma((6,)),
            dma((GROUPS,)), dma((GROUPS,)),
            dma((GROUPS,)), dma((GROUPS,)),
            dma((GROUPS,)), dma((GROUPS,)),
            dma((1,)), dma((1,)),
            dma((GROUPS,)), dma((GROUPS,)),
            dma((GROUPS,)), dma((GROUPS,)),
        ],
        compiler_params=pltpu.CompilerParams(
            collective_id=0, has_side_effects=True, vmem_limit_bytes=VMEM_LIMIT
        ),
        cost_estimate=pl.CostEstimate(
            flops=20 * 10**9, bytes_accessed=10 * 10**6, transcendentals=9 * 10**6
        ),
        name="routed_ranking",
    )(
        candidates,
        cand_dest.reshape(1, ROWS),
        cand_slot.reshape(1, ROWS),
        hist_len,
        k_cache,
        v_cache,
        in_gain.reshape(1, D),
        w_uvqk,
        attn_gain.reshape(1, W),
        w_out,
    )


def solution(mesh):
    return jax.shard_map(
        body,
        mesh=mesh,
        in_specs=(
            P("users", "mp"),
            P("users", None),
            P("users"),
            P("users", None),
            P("users", None, "mp"),
            P("users", None, "mp"),
            P(),
            P(None, None, "mp"),
            P("mp"),
            P(None, "mp"),
        ),
        out_specs=P("users", "mp"),
        check_vma=False,
    )
```

```python
import functools
import math

import jax
import jax.numpy as jnp
from jax import lax
from jax.experimental import pallas as pl
from jax.experimental.pallas import tpu as pltpu
from jax.sharding import PartitionSpec as P

MESH = pl.DeviceIdType.MESH
D = 1024
W = 512
HD = 128
HEADS_HERE = W // HD
HLEN = 512
ROWS = 1024
PEERS = 64
SIDE = 4
CAP = 32
SLOTS = PEERS * CAP
GROUP = 8
GROUPS = PEERS // GROUP
GR = GROUP * CAP
STEP = 37
STEP_INV = 45
LAG = 5
HOLD = 3
ORDER = 'EFG'
EPS = 1e-05
VMEM_LIMIT = 54 * 2**20
ABL = CAP
SCALE = 1.0 / math.sqrt(HD)
F32 = jnp.float32
BF16 = jnp.bfloat16


def silu(x):
    t = 0.5 * x
    return t + t * jnp.tanh(t)


def digits(k):
    return k % SIDE, (k // SIDE) % SIDE, k // (SIDE * SIDE)


def ahead(me, j):
    x, y, z = digits(me)
    a, b, c = digits((j * STEP) % PEERS)
    return ((z + c) % SIDE) * SIDE * SIDE + ((y + b) % SIDE) * SIDE + (x + a) % SIDE


def behind(me, j):
    x, y, z = digits(me)
    a, b, c = digits((j * STEP) % PEERS)
    return (
        ((z + SIDE - c) % SIDE) * SIDE * SIDE
        + ((y + SIDE - b) % SIDE) * SIDE
        + (x + SIDE - a) % SIDE
    )


def mirrored(j):
    a, b, c = digits((j * STEP) % PEERS)
    k = ((SIDE - c) % SIDE) * SIDE * SIDE + ((SIDE - b) % SIDE) * SIDE + (SIDE - a) % SIDE
    return (k * STEP_INV) % PEERS


def kernel(
    x_hbm, dest_ref, slot_ref, hist_ref, k_hbm, v_hbm, in_gain_ref, w_hbm, attn_gain_ref, wout_hbm,
    out_ref,
    x_v, w_raw, w_v, wout_v, k_v, v_v, v01, fs_row, fs_col, meta, metar, theirs, mask_in, inv_len, gain_v,
    xs_own, xs_peer, h_v, q_send, q_recv, a_send, back, u_v, self_v, st_send, st_recv,
    y_own, y_peer, acc,
    load_sem, x_ssem, x_rsem, q_ssem, q_rsem, a_ssem, a_rsem, m_ssem, m_rsem, s_ssem, s_rsem,
    y_ssem, y_rsem,
):
    me = lax.axis_index("users")
    mp = lax.axis_index("mp")
    other = 1 - mp
    own_at = pl.multiple_of(mp * W, W)
    peer_at = pl.multiple_of(other * W, W)

    barrier = pltpu.get_barrier_semaphore()

    def greet(j, carry):
        pl.semaphore_signal(barrier, inc=1, device_id=(ahead(me, j), mp), device_id_type=MESH)
        return carry

    pl.semaphore_signal(barrier, inc=1, device_id=(me, other), device_id_type=MESH)
    lax.fori_loop(1, PEERS, greet, 0)

    loads = [
        pltpu.make_async_copy(x_hbm, x_v, load_sem.at[0]),
        pltpu.make_async_copy(w_hbm, w_raw, load_sem.at[1]),
        pltpu.make_async_copy(wout_hbm.at[pl.ds(own_at, W)], wout_v.at[pl.ds(0, W)], load_sem.at[2]),
        pltpu.make_async_copy(k_hbm, k_v, load_sem.at[3]),
        pltpu.make_async_copy(v_hbm, v_v, load_sem.at[4]),
    ]
    loads.append(
        pltpu.make_async_copy(wout_hbm.at[pl.ds(peer_at, W)], wout_v.at[pl.ds(W, W)], load_sem.at[5])
    )
    for c in loads:
        c.start()

    dest = dest_ref[...]
    slot = slot_ref[...]
    mx, my, mz = digits(me)
    kx = ((dest & 3) + (SIDE - mx)) & 3
    ky = (((dest >> 2) & 3) + (SIDE - my)) & 3
    kz = ((dest >> 4) + (SIDE - mz)) & 3
    number = ((kx + 4 * ky + 16 * kz) * STEP_INV) & (PEERS - 1)
    key = 2 * number + slot
    hot = (lax.broadcasted_iota(jnp.int32, (2 * PEERS, ROWS), 0) == key).astype(F32)
    before = jnp.zeros((2 * PEERS, 256), F32)
    pos_parts = []
    tri = (
        lax.broadcasted_iota(jnp.int32, (256, 256), 0)
        < lax.broadcasted_iota(jnp.int32, (256, 256), 1)
    ).astype(F32).astype(BF16)
    count = jnp.zeros((2 * PEERS, 1), F32)
    for b in range(ROWS // 256):
        part = hot[:, b * 256 : (b + 1) * 256]
        before = jnp.dot(part.astype(BF16), tri, preferred_element_type=F32) + count
        pos_parts.append(jnp.sum(before * part, axis=0, keepdims=True))
        count = count + jnp.sum(part, axis=1, keepdims=True)
    pos = jnp.concatenate(pos_parts, axis=1)
    fs = (number * CAP).astype(F32) + jnp.where(slot == 0, pos, (CAP - 1) - pos)
    fs_row[...] = jnp.broadcast_to(fs, (8, ROWS))

    def rows_of(g):
        return pl.ds(pl.multiple_of(g * GR, GR), GR)

    def chunk_of(j):
        return pl.ds(pl.multiple_of(j * CAP, CAP), CAP)

    def abl_of(j):
        return pl.ds(pl.multiple_of(j * CAP, CAP), ABL)

    def x_copy(g):
        return pltpu.make_async_remote_copy(
            src_ref=xs_own.at[rows_of(g)], dst_ref=xs_peer.at[rows_of(g)],
            send_sem=x_ssem.at[g], recv_sem=x_rsem.at[g],
            device_id=(me, other), device_id_type=MESH,
        )

    def q_copy(g, j):
        return pltpu.make_async_remote_copy(
            src_ref=q_send.at[abl_of(j)], dst_ref=q_recv.at[abl_of(j)],
            send_sem=q_ssem.at[g], recv_sem=q_rsem.at[g],
            device_id=(ahead(me, j), mp), device_id_type=MESH,
        )

    def a_copy(g, j):
        return pltpu.make_async_remote_copy(
            src_ref=a_send.at[abl_of(j)], dst_ref=back.at[abl_of(j)],
            send_sem=a_ssem.at[g], recv_sem=a_rsem.at[g],
            device_id=(behind(me, j), mp), device_id_type=MESH,
        )

    def s_copy(g):
        return pltpu.make_async_remote_copy(
            src_ref=st_send.at[rows_of(g)], dst_ref=st_recv.at[rows_of(g)],
            send_sem=s_ssem.at[g], recv_sem=s_rsem.at[g],
            device_id=(me, other), device_id_type=MESH,
        )

    def y_copy(g):
        return pltpu.make_async_remote_copy(
            src_ref=y_own.at[rows_of(g)], dst_ref=y_peer.at[rows_of(g)],
            send_sem=y_ssem.at[g], recv_sem=y_rsem.at[g],
            device_id=(me, other), device_id_type=MESH,
        )

    def m_copy(j):
        return pltpu.make_async_remote_copy(
            src_ref=meta.at[j], dst_ref=metar.at[j],
            send_sem=m_ssem.at[0], recv_sem=m_rsem.at[0],
            device_id=(ahead(me, j), mp), device_id_type=MESH,
        )

    def gather(g):
        slots = lax.broadcasted_iota(jnp.int32, (GR, ROWS), 0).astype(F32) + (g * GR).astype(F32)
        pick = jnp.where(slots == fs_row[0:1, :], 1.0, 0.0).astype(BF16)
        xs_own[rows_of(g), :] = jnp.dot(pick, x_v[...], preferred_element_type=F32).astype(BF16)

    def norm_and_query(g):
        x_copy(g).wait_recv()
        xo = xs_own[rows_of(g), :].astype(F32)
        xp = xs_peer[rows_of(g), :].astype(F32)
        xf = jnp.concatenate([xo, xp], axis=1)
        mean = jnp.sum(xf, axis=1, keepdims=True) * (1.0 / D)
        c = xf - mean
        var = jnp.sum(c * c, axis=1, keepdims=True) * (1.0 / D)
        h = (c * lax.rsqrt(var + EPS) * gain_v[...]).astype(BF16)
        h_v[rows_of(g), :] = h
        q_send[rows_of(g), :] = silu(jnp.dot(h, w_v[2], preferred_element_type=F32)).astype(BF16)

    def send_queries(g):
        lo = jnp.where(g == 0, 1, g * GROUP)

        def one(j, carry):
            q_copy(g, j).start()
            return carry

        lax.fori_loop(lo, (g + 1) * GROUP, one, 0)

    def project_rest(g):
        h = h_v[rows_of(g), :]
        u_v[rows_of(g), :] = silu(jnp.dot(h, w_v[0], preferred_element_type=F32)).astype(BF16)
        v = silu(jnp.dot(h, w_v[1], preferred_element_type=F32)).astype(BF16).astype(F32)
        k = silu(jnp.dot(h, w_v[3], preferred_element_type=F32)).astype(BF16).astype(F32)
        q = q_send[rows_of(g), :].astype(F32)
        qk = q * k
        for n in range(HEADS_HERE):
            cols = slice(n * HD, (n + 1) * HD)
            s = jnp.sum(qk[:, cols], axis=1, keepdims=True) * SCALE
            sw = silu(s).astype(BF16).astype(F32)
            self_v[rows_of(g), cols] = sw * v[:, cols] * inv_len[rows_of(g), :]

    def attend(g):
        m1 = mask_in[rows_of(g), :]
        m0 = 1.0 - m1
        rs = m0 * (1.0 / (len0 + 1.0)) + m1 * (1.0 / (len1 + 1.0))
        for n in range(HEADS_HERE):
            cols = slice(n * HD, (n + 1) * HD)
            qf = q_recv[rows_of(g), cols].astype(F32)
            q01 = jnp.concatenate([(qf * m0).astype(BF16), (qf * m1).astype(BF16)], axis=1)
            k01 = jnp.concatenate([k_v[0, :, cols], k_v[1, :, cols]], axis=1)
            s = lax.dot_general(q01, k01, (((1,), (1,)), ((), ())), preferred_element_type=F32)
            t = s * (0.5 * SCALE)
            wts = (t + t * jnp.tanh(t)).astype(BF16)
            o = jnp.dot(wts, v01[n], preferred_element_type=F32)
            a = (o[:, :HD] * m0 + o[:, HD:] * m1) * rs
            a_send[rows_of(g), cols] = a.astype(BF16)

    def send_back(g):
        lo = jnp.where(g == 0, 1, g * GROUP)

        def one(j, carry):
            a_copy(g, j).start()
            return carry

        lax.fori_loop(lo, (g + 1) * GROUP, one, 0)

    def finish_sums(g):
        a = back[rows_of(g), :].astype(F32) + self_v[rows_of(g), :]
        mean = jnp.sum(a, axis=1, keepdims=True) * (1.0 / W)
        c = a - mean
        m2 = jnp.sum(c * c, axis=1, keepdims=True)
        self_v[rows_of(g), :] = a
        lanes = lax.broadcasted_iota(jnp.int32, (GR, HD), 1)
        st_send[rows_of(g), :] = jnp.where(lanes < 64, mean, m2)
        s_copy(g).start()

    def normalize(g):
        s_copy(g).wait_recv()
        so = st_send[rows_of(g), :]
        sp = st_recv[rows_of(g), :]
        mo, mp_ = so[:, 0:1], sp[:, 0:1]
        mean = 0.5 * (mo + mp_)
        gap = mo - mp_
        var = (so[:, 64:65] + sp[:, 64:65] + (0.5 * W) * gap * gap) * (1.0 / D)
        y = (
            (self_v[rows_of(g), :] - mean)
            * lax.rsqrt(var + EPS)
            * attn_gain_ref[...]
            * u_v[rows_of(g), :].astype(F32)
        )
        y_own[rows_of(g), :] = y.astype(BF16)
        y_copy(g).start()

    def output(g):
        y_copy(g).wait_recv()
        y = jnp.concatenate([y_own[rows_of(g), :], y_peer[rows_of(g), :]], axis=1)
        p = jnp.dot(y, wout_v[...], preferred_element_type=F32)
        fin = (xs_own[rows_of(g), :].astype(F32) + p).astype(BF16)
        base = (g * GR).astype(F32)
        lanes = lax.broadcasted_iota(jnp.int32, (ROWS, HD), 1).astype(F32) + base
        f = fs_col[...]
        pick = jnp.concatenate(
            [jnp.where(f == lanes + float(n * HD), 1.0, 0.0).astype(BF16) for n in range(GR // HD)],
            axis=1,
        )
        acc[...] += jnp.dot(pick, fin, preferred_element_type=F32)

    loads[0].wait()
    gather(jnp.int32(0))
    pl.semaphore_wait(barrier, PEERS)
    x_copy(0).start()

    fs_col[...] = jnp.broadcast_to(fs, (HD, ROWS)).T
    same = lax.broadcasted_iota(jnp.int32, (PEERS, ROWS), 0) == number
    first = jnp.sum(jnp.where(same & (slot == 0), 1.0, 0.0), axis=1, keepdims=True)
    hist = hist_ref[...].astype(F32)
    len0, len1 = hist[:, 0:1], hist[:, 1:2]
    lane = lax.broadcasted_iota(jnp.int32, (PEERS, HD), 1)
    meta_rows = jnp.where(lane < 64, first, jnp.where(lane < 96, len0, len1))
    meta[...] = meta_rows.reshape(PEERS, 1, HD)
    metar[0] = meta[0]
    gain_v[...] = jnp.concatenate(
        [in_gain_ref[:, pl.ds(own_at, W)], in_gain_ref[:, pl.ds(peer_at, W)]], axis=1
    )
    acc[...] = jnp.zeros_like(acc)

    def send_meta(j, carry):
        m_copy(j).start()
        return carry

    lax.fori_loop(1, PEERS, send_meta, 0)

    def regroup(b, carry):
        src = pl.ds(pl.multiple_of(b * 64, 64), 64)
        dst = pl.ds(pl.multiple_of((b * 64 + mp * W) % D, 64), 64)
        w_v[:, dst, :] = jnp.swapaxes(w_raw[src], 0, 1)
        return carry

    loads[1].wait()
    lax.fori_loop(0, D // 64, regroup, 0)

    def head(i, carry):
        @pl.when(i < GROUPS)
        def _():
            gather(i)
            x_copy(i).start()

        norm_and_query(i - 1)

        @pl.when(i == 1)
        def _():
            q_recv[pl.ds(0, CAP), :] = q_send[pl.ds(0, CAP), :]

        send_queries(i - 1)
        return carry

    lax.fori_loop(1, GROUPS + 1, head, 0)

    for c in loads[2:]:
        c.wait()
    place = lax.broadcasted_iota(jnp.int32, (HLEN, W), 0).astype(F32)
    for user, length in ((0, len0), (1, len1)):
        kept = jnp.where(place < length, v_v[user].astype(F32), 0.0).astype(BF16)
        for n in range(HEADS_HERE):
            v01[n, :, user * HD : (user + 1) * HD] = kept[:, n * HD : (n + 1) * HD]

    pltpu.make_async_copy(
        metar.at[pl.ds(1, PEERS - 1)], metar.at[pl.ds(1, PEERS - 1)], m_rsem.at[0]
    ).wait()
    for j in range(PEERS):
        theirs[j] = metar[mirrored(j)]
    in_chunk = lax.broadcasted_iota(jnp.int32, (PEERS, CAP, HD), 1).astype(F32)
    mask_in[...] = jnp.where(in_chunk >= metar[...][:, :, 0:1], 1.0, 0.0).reshape(SLOTS, HD)
    inv = 1.0 / (theirs[...] + 1.0)
    inv_len[...] = jnp.where(
        in_chunk >= meta[...][:, :, 0:1], inv[:, :, 96:97], inv[:, :, 64:65]
    ).reshape(SLOTS, HD)

    def wait_group(buf, sem, g):
        @pl.when(g == 0)
        def _():
            rows = pl.ds(ABL, (GROUP-1)*ABL)
            pltpu.make_async_copy(buf.at[rows], buf.at[rows], sem.at[0]).wait()

        @pl.when(g > 0)
        def _():
            rows = pl.ds(pl.multiple_of(g * GR, GR), GROUP * ABL)
            pltpu.make_async_copy(buf.at[rows], buf.at[rows], sem.at[g]).wait()

    def body(i, carry):
        @pl.when(i < GROUPS)
        def _():
            project_rest(i)
            wait_group(q_recv, q_rsem, i)
            attend(i)

            @pl.when(i == 0)
            def _():
                back[pl.ds(0, CAP), :] = a_send[pl.ds(0, CAP), :]

        @pl.when(jnp.logical_and(i >= HOLD, i < GROUPS))
        def _():
            send_back(i - HOLD)

        @pl.when(i == GROUPS - 1)
        def _():
            for g in range(GROUPS - HOLD, GROUPS):
                send_back(jnp.int32(g))

        def out_step():
            @pl.when(jnp.logical_and(i >= LAG + 2, i < GROUPS + LAG + 2))
            def _():
                output(i - LAG - 2)

        def norm_step():
            @pl.when(jnp.logical_and(i >= LAG + 1, i < GROUPS + LAG + 1))
            def _():
                normalize(i - LAG - 1)

        def sum_step():
            @pl.when(jnp.logical_and(i >= LAG, i < GROUPS + LAG))
            def _():
                wait_group(back, a_rsem, i - LAG)
                finish_sums(i - LAG)

        steps = dict(E=sum_step, F=norm_step, G=out_step)
        for name in ORDER:
            steps[name]()

        return carry

    lax.fori_loop(0, GROUPS + LAG + 2, body, 0)
    out_ref[...] = acc[...].astype(BF16)

    def drain(g, carry):
        x_copy(g).wait_send()
        s_copy(g).wait_send()
        y_copy(g).wait_send()
        wait_group(q_send, q_ssem, g)
        wait_group(a_send, a_ssem, g)
        return carry

    lax.fori_loop(0, GROUPS, drain, 0)
    pltpu.make_async_copy(
        meta.at[pl.ds(1, PEERS - 1)], meta.at[pl.ds(1, PEERS - 1)], m_ssem.at[0]
    ).wait()


def body(
    candidates, cand_dest, cand_slot, hist_len, k_cache, v_cache, in_gain, w_uvqk, attn_gain, w_out
):
    vmem = pl.BlockSpec(memory_space=pltpu.VMEM)
    hbm = pl.BlockSpec(memory_space=pl.ANY)
    dma = pltpu.SemaphoreType.DMA
    return pl.pallas_call(
        kernel,
        out_shape=jax.ShapeDtypeStruct((ROWS, W), BF16),
        in_specs=[hbm, vmem, vmem, vmem, hbm, hbm, vmem, hbm, vmem, hbm],
        out_specs=vmem,
        scratch_shapes=[
            pltpu.VMEM((ROWS, W), BF16),
            pltpu.VMEM((D, 4, W), BF16),
            pltpu.VMEM((4, D, W), BF16),
            pltpu.VMEM((D, W), BF16),
            pltpu.VMEM((2, HLEN, W), BF16),
            pltpu.VMEM((2, HLEN, W), BF16),
            pltpu.VMEM((HEADS_HERE, HLEN, 2 * HD), BF16),
            pltpu.VMEM((8, ROWS), F32),
            pltpu.VMEM((ROWS, HD), F32),
            pltpu.VMEM((PEERS, 1, HD), F32),
            pltpu.VMEM((PEERS, 1, HD), F32),
            pltpu.VMEM((PEERS, 1, HD), F32),
            pltpu.VMEM((SLOTS, HD), F32),
            pltpu.VMEM((SLOTS, HD), F32),
            pltpu.VMEM((1, D), F32),
            pltpu.VMEM((SLOTS, W), BF16),
            pltpu.VMEM((SLOTS, W), BF16),
            pltpu.VMEM((SLOTS, D), BF16),
            pltpu.VMEM((SLOTS, W), BF16),
            pltpu.VMEM((SLOTS, W), BF16),
            pltpu.VMEM((SLOTS, W), BF16),
            pltpu.VMEM((SLOTS, W), BF16),
            pltpu.VMEM((SLOTS, W), BF16),
            pltpu.VMEM((SLOTS, W), F32),
            pltpu.VMEM((SLOTS, HD), F32),
            pltpu.VMEM((SLOTS, HD), F32),
            pltpu.VMEM((SLOTS, W), BF16),
            pltpu.VMEM((SLOTS, W), BF16),
            pltpu.VMEM((ROWS, W), F32),
            dma((6,)),
            dma((GROUPS,)), dma((GROUPS,)),
            dma((GROUPS,)), dma((GROUPS,)),
            dma((GROUPS,)), dma((GROUPS,)),
            dma((1,)), dma((1,)),
            dma((GROUPS,)), dma((GROUPS,)),
            dma((GROUPS,)), dma((GROUPS,)),
        ],
        compiler_params=pltpu.CompilerParams(
            collective_id=0, has_side_effects=True, vmem_limit_bytes=VMEM_LIMIT
        ),
        cost_estimate=pl.CostEstimate(
            flops=20 * 10**9, bytes_accessed=10 * 10**6, transcendentals=9 * 10**6
        ),
        name="routed_ranking",
    )(
        candidates,
        cand_dest.reshape(1, ROWS),
        cand_slot.reshape(1, ROWS),
        hist_len,
        k_cache,
        v_cache,
        in_gain.reshape(1, D),
        w_uvqk,
        attn_gain.reshape(1, W),
        w_out,
    )


def solution(mesh):
    return jax.shard_map(
        body,
        mesh=mesh,
        in_specs=(
            P("users", "mp"),
            P("users", None),
            P("users"),
            P("users", None),
            P("users", None, "mp"),
            P("users", None, "mp"),
            P(),
            P(None, None, "mp"),
            P("mp"),
            P(None, "mp"),
        ),
        out_specs=P("users", "mp"),
        check_vma=False,
    )
```
